128 devices in a mesh: ctx: 16 (over z, y_hi, core), tp: 8 (over x, y_lo).
Axes of the slice: x: 4, y: 4 (y_hi: 2, y_lo: 2; y = y_hi * 2 + y_lo), z: 4, core: 2. Of those that a mesh axis runs over, the one named last changes fastest.
Arguments:
- prompt: bfloat16 [8192, 5120], P('ctx'), may hold values from -6 to 6
- norm_gain: float32 [5120], replicated, may hold values from 0.1 to 1.9
- w_query: bfloat16 [5120, 8192], P(None, 'tp')
- w_key: bfloat16 [5120, 1024], P(None, 'tp')
- w_value: bfloat16 [5120, 1024], P(None, 'tp'), may hold values from -0.078125 to 0.078125
- query_gain: float32 [128], replicated, may hold values from 1.5 to 4
- key_gain: float32 [128], replicated, may hold values from 1.5 to 4
- table: bfloat16 [77824, 5120], P(('ctx', 'tp')), may hold values from -6 to 6
- sampled: int32 [16, 4], replicated, may hold values from 0 to 77823
Outputs:
- prompt_out: bfloat16 [8192, 8192], P('ctx', 'tp')
- decoded: bfloat16 [16, 4, 8192], P('ctx', None, 'tp')
The draws below stay inside these ranges and needn't reach their ends.
All inputs are finite; a program needn't handle non-finite values.
Results may differ from the reference program's by a relative error of at most 0.012.
The reference program's roundings to bfloat16 on the way (of `normed`, `values` and `weights`) count: a program that leaves them out, or rounds other values in their place, can miss the bound.
Values may be sent and summed in bfloat16 or wider, within the bound.
A program may use at most 128 MiB of HBM per device.

```python
import math
import jax
import jax.numpy as jnp
from jax import lax

D = 5120
HQ = 64
KVH = 8
HEAD = 128
VOCAB = 77824
STEPS = 4
L = 8192
SAMPLES = 16


def shared_keys(key):
    return jax.random.normal(key, (D, KVH * HEAD), jnp.float32) * D ** (-0.5)


def draw_w_key(key, part):
    return shared_keys(key).astype(jnp.bfloat16)


def draw_w_query(key, part):
    key = jax.random.fold_in(key, 11)
    noise = jax.random.normal(key, (D, KVH, HQ // KVH, HEAD), jnp.float32) * D ** (-0.5)
    return noise.reshape(D, HQ * HEAD).astype(jnp.bfloat16)


def draw_query_gain(key, part):
    key = jax.random.fold_in(key, 21)
    return jax.random.uniform(key, (HEAD,), jnp.float32, 1.5, 3.0)


def draw_key_gain(key, part):
    key = jax.random.fold_in(key, 22)
    return jax.random.uniform(key, (HEAD,), jnp.float32, 1.5, 3.0)


def with_ends(array, rng, least, high):
    longest = array.shape.index(max(array.shape))
    spots = []
    for shift in (0, 1):
        where = [jax.random.randint(jax.random.fold_in(rng, axis), (), 0, length) for axis, length in enumerate(array.shape)]
        where[longest] = (where[longest] + shift) % array.shape[longest]
        spots.append(tuple(where))
    return array.at[spots[0]].set(least).at[spots[1]].set(high)


def steps_of(stream_key, dims, split, low, high):
    def one(position, blocks):
        steps = jax.random.uniform(jax.random.fold_in(jax.random.fold_in(stream_key, 6), position), (blocks,), jnp.float32, low / len(split), high / len(split))
        return jnp.repeat(jnp.exp(steps), dims[position] // blocks).reshape((-1,) + (1,) * (len(dims) - position - 1))

    level = one(*split[0])
    for cut in split[1:]:
        level = level * one(*cut)
    return level


def gaussian(stream_key, extent, scale, most, pieces=(), kind=jnp.bfloat16):
    level = steps_of(stream_key, extent, pieces, -0.22, 0.18) if pieces else 1.0
    values = jax.random.normal(stream_key, extent, jnp.float32) * scale * level
    return jnp.minimum(jnp.maximum(values, -most), most).astype(kind)


def setup_inputs(seed: int = 0) -> dict:
    key_of = jax.random.split(jax.random.key(seed), 10)
    prompt = gaussian(key_of[0], (L, D), 1.0, 6.0, ((0, 16),))
    norm_gain = jnp.clip(1.0 + 0.18 * jax.random.normal(key_of[1], (D,), jnp.float32), 0.1, 1.9)
    w_query = draw_w_query(jax.random.fold_in(key_of[9], 71), 0)
    w_key = draw_w_key(jax.random.fold_in(key_of[9], 71), 0)
    w_value = gaussian(key_of[4], (D, KVH * HEAD), D ** -0.5, 0.078125, ((1, 8),))
    query_gain = draw_query_gain(jax.random.fold_in(key_of[9], 71), 0)
    key_gain = draw_key_gain(jax.random.fold_in(key_of[9], 71), 0)
    table = gaussian(key_of[7], (VOCAB, D), 1.0, 6.0, ((0, 128),))
    sampled = with_ends(jax.random.randint(key_of[8], (SAMPLES, STEPS), 0, VOCAB), jax.random.fold_in(key_of[8], 1), 0, VOCAB - 1).astype(jnp.int32)
    return {"prompt": prompt, "norm_gain": norm_gain, "w_query": w_query, "w_key": w_key, "w_value": w_value, "query_gain": query_gain, "key_gain": key_gain, "table": table, "sampled": sampled}


EPS = 1e-06
THETA = 1000000.0

def rms_scale(values, gain):
    mean_square = lax.optimization_barrier(jnp.mean(values * values, axis=-1, keepdims=True))
    return values * lax.rsqrt(mean_square + EPS) * gain

def rotate(values, positions):
    half = values.shape[-1] // 2
    freqs = THETA ** (-jnp.arange(half, dtype=jnp.float32) / half)
    angles = positions.astype(jnp.float32)[:, None] * freqs[None, :]
    cosine = jnp.cos(angles)[:, None, :]
    sine = jnp.sin(angles)[:, None, :]
    first = values[..., :half]
    second = values[..., half:]
    return jnp.concatenate([first * cosine - second * sine, second * cosine + first * sine], axis=-1)

def project(hidden, positions, norm_gain, w_query, w_key, w_value, query_gain, key_gain):
    count = hidden.shape[0]
    normed = rms_scale(hidden, norm_gain).astype(jnp.bfloat16)
    query_raw = jnp.dot(normed, w_query, preferred_element_type=jnp.float32).reshape(count, -1, HEAD)
    key_raw = jnp.dot(normed, w_key, preferred_element_type=jnp.float32).reshape(count, -1, HEAD)
    values = jnp.dot(normed, w_value, preferred_element_type=jnp.float32).astype(jnp.bfloat16).reshape(count, -1, HEAD)
    queries = rotate(rms_scale(query_raw, query_gain), positions).astype(jnp.bfloat16)
    keys = rotate(rms_scale(key_raw, key_gain), positions).astype(jnp.bfloat16)
    return (queries, keys, values)

def attend(queries, keys, values, mask):
    scores = jnp.einsum('qhgd,khd->hgqk', queries.astype(jnp.float32), keys.astype(jnp.float32)) * HEAD ** (-0.5)
    top = lax.optimization_barrier(jnp.max(jnp.where(mask, scores, -1e+30), axis=-1, keepdims=True))
    raw_weights = jnp.where(mask, jnp.exp(scores - top), 0.0)
    total = lax.optimization_barrier(jnp.sum(raw_weights, axis=-1))
    weights = lax.optimization_barrier(raw_weights.astype(jnp.bfloat16))
    mixed = jnp.einsum('hgqk,khd->hgqd', weights.astype(jnp.float32), values.astype(jnp.float32))
    return jnp.transpose(mixed / total[..., None], (2, 0, 1, 3))

def reference(prompt, norm_gain, w_query, w_key, w_value, query_gain, key_gain, table, sampled):
    group = HQ // KVH
    positions = jnp.arange(L, dtype=jnp.int32)
    queries, keys, values = project(prompt.astype(jnp.float32), positions, norm_gain, w_query, w_key, w_value, query_gain, key_gain)
    grouped = queries.reshape(L, KVH, group, HEAD)
    block = math.gcd(L, 128)

    def prompt_block(index):
        start = index * block
        part = lax.dynamic_slice_in_dim(grouped, start, block, 0)
        query_pos = start + jnp.arange(block, dtype=jnp.int32)
        mask = positions[None, :] <= query_pos[:, None]
        return attend(part, keys, values, mask)
    blocks = lax.map(prompt_block, jnp.arange(L // block, dtype=jnp.int32))
    prompt_out = blocks.reshape(L, HQ * HEAD).astype(jnp.bfloat16)
    step_pos = L + jnp.arange(STEPS, dtype=jnp.int32)
    causal = jnp.arange(STEPS, dtype=jnp.int32)[None, :] <= jnp.arange(STEPS, dtype=jnp.int32)[:, None]
    mask = jnp.concatenate([jnp.ones((STEPS, L), dtype=bool), causal], axis=1)

    def sample_run(ids):
        hidden = table[ids].astype(jnp.float32)
        step_q, step_k, step_v = project(hidden, step_pos, norm_gain, w_query, w_key, w_value, query_gain, key_gain)
        all_keys = jnp.concatenate([keys, step_k], axis=0)
        all_values = jnp.concatenate([values, step_v], axis=0)
        result = attend(step_q.reshape(STEPS, KVH, group, HEAD), all_keys, all_values, mask)
        return result.reshape(STEPS, HQ * HEAD)
    decoded = lax.map(sample_run, sampled).astype(jnp.bfloat16)
    return (prompt_out, decoded)
```

```python
import functools

import jax
import jax.numpy as jnp
import numpy as np
from jax import lax
from jax.experimental import pallas as pl
from jax.experimental.pallas import tpu as pltpu
from jax.sharding import PartitionSpec as P

MESH = pl.DeviceIdType.MESH
EPS = 1e-06
THETA = 1000000.0
HD = 128
ROWS = 512
D = 5120
PAIR = 2 * ROWS
HEADS = 8
NCTX = 16
NTP = 8
VROWS = 608
PIECE = D // NTP
SCALE = HD ** (-0.5) * 1.4426950408889634
LOW = -1e30
GROUP = 10
SPARE = 12
ACC = HD + 16


def rope_tables(prompt_len):
    half = HD // 2
    freqs = THETA ** (-np.arange(half, dtype=np.float64) / half)
    freqs = np.concatenate([freqs, freqs])[None, :]
    sign = np.concatenate([-np.ones(half), np.ones(half)])[None, :]
    near = np.arange(ROWS, dtype=np.float64)[:, None] * freqs
    far = (np.arange(prompt_len // ROWS + 1, dtype=np.float64) * ROWS)[:, None] * freqs
    tables = (np.cos(near), np.sin(near) * sign, np.cos(far), np.sin(far) * sign)
    return [t.astype(np.float32) for t in tables]


def kernel(
    prompt, gain, w_query, w_key, w_value, q_gain, k_gain, table, ids, near_c, near_s, far_c, far_s, spread,
    out, dec,
    x, wq, wkv, tab, q, kbuf, vbuf, acc, top, es, er, eb, ec, eh, xs, qd, accd, topd, fsend, frecv,
    load_sem, wq_sem, ks, kr, vs, vr, e1s, e1r, e2s, e2r, e3s, e3r, qs, qr, fs, fr,
):
    ctx = lax.axis_index("ctx")
    tp = lax.axis_index("tp")
    chip = ctx // 2
    core = ctx % 2
    z = ctx // 4
    yh = chip % 2

    def remote(src, dst, send, recv, to_ctx, to_tp):
        return pltpu.make_async_remote_copy(
            src_ref=src, dst_ref=dst, send_sem=send, recv_sem=recv,
            device_id=(to_ctx, to_tp), device_id_type=MESH,
        )

    prompt_loads = []
    for n in range(4):
        rows = pl.ds(n * 128, 128)
        prompt_loads.append(pltpu.make_async_copy(prompt.at[rows], x.at[rows], load_sem.at[n]))
    key_load = pltpu.make_async_copy(w_key, wkv.at[:, pl.ds(0, HD)], load_sem.at[4])
    value_load = pltpu.make_async_copy(w_value, wkv.at[:, pl.ds(HD, HD)], load_sem.at[5])
    table_load = pltpu.make_async_copy(table, tab, load_sem.at[6])
    query_loads = []
    for n in range(2):
        cols = pl.ds((1 - n) * 512, 512)
        query_loads.append(pltpu.make_async_copy(w_query.at[:, cols], wq.at[:, cols], wq_sem.at[n]))
    for load in (*prompt_loads, key_load, value_load, query_loads[0], table_load, query_loads[1]):
        load.start()

    barrier = pltpu.get_barrier_semaphore()

    @pl.loop(1, NCTX)
    def _(i):
        pl.semaphore_signal(barrier, inc=1, device_id=((ctx + i) % NCTX, tp), device_id_type=MESH)

    @pl.loop(1, NTP)
    def _(i):
        pl.semaphore_signal(barrier, inc=1, device_id=(ctx, (tp + i) % NTP), device_id_type=MESH)

    def normed(rows_f32):
        mean_square = jnp.mean(rows_f32 * rows_f32, axis=-1, keepdims=True)
        return (rows_f32 * lax.rsqrt(mean_square + EPS) * gain[...]).astype(jnp.bfloat16)

    for n in range(4):
        prompt_loads[n].wait()

        @pl.loop(0, 8, unroll=2)
        def _(i):
            rows = pl.ds(pl.multiple_of(n * 128 + i * 16, 16), 16)
            x[rows, :] = normed(x[rows, :].astype(jnp.float32))

    def rotated(raw, head_gain, cosine, sine):
        mean_square = jnp.mean(raw * raw, axis=-1, keepdims=True)
        y = raw * lax.rsqrt(mean_square + EPS) * head_gain
        return (y * cosine + pltpu.roll(y, HD // 2, 1) * sine).astype(jnp.bfloat16)

    base_c, base_s = far_c[pl.ds(ctx, 1), :], far_s[pl.ds(ctx, 1), :]
    cosine = near_c[...] * base_c - near_s[...] * base_s
    sine = near_s[...] * base_c + near_c[...] * base_s

    key_load.wait()
    value_load.wait()
    kv = jnp.dot(x[...], wkv[...], preferred_element_type=jnp.float32)
    kbuf[ctx] = rotated(kv[:, :HD], k_gain[...], cosine, sine)
    vbuf[ctx] = kv[:, HD:].T.astype(jnp.bfloat16)

    pl.semaphore_wait(barrier, NCTX + NTP - 2)

    def block(zz, yy, cc):
        return zz * 4 + yy * 2 + cc

    zp, zm, z2 = (z + 1) % 4, (z + 3) % 4, (z + 2) % 4
    sib = block(z, yh, 1 - core)
    up, down, across = block(zp, yh, core), block(zm, yh, core), block(z, 1 - yh, core)
    sent = []

    def send(kind, b, to):
        if kind == "k":
            n = sum(1 for s in sent if s[0] == "k")
            copy = remote(kbuf.at[b], kbuf.at[b], ks.at[n], kr.at[b], to, tp)
        else:
            n = sum(1 for s in sent if s[0] == "v")
            copy = remote(vbuf.at[b], vbuf.at[b], vs.at[n], vr.at[b], to, tp)
        copy.start()
        sent.append((kind, copy))

    def arrived(kind, b):
        if kind == "k":
            remote(kbuf.at[b], kbuf.at[b], ks.at[0], kr.at[b], sib, tp).wait_recv()
        else:
            remote(vbuf.at[b], vbuf.at[b], vs.at[0], vr.at[b], sib, tp).wait_recv()

    def hop_own():
        for to in (across, up, down, sib):
            send("k", ctx, to)
            send("v", ctx, to)

    def hop_ring(yy):
        left, right = block(zm, yy, core), block(zp, yy, core)
        arrived("k", left)
        send("k", left, up)
        arrived("v", right)
        send("v", right, down)
        arrived("v", left)
        arrived("k", right)
        for b in (left, right):
            send("k", b, sib)
            send("v", b, sib)

    def hop_across():
        b = across
        arrived("k", b)
        arrived("v", b)
        for to in (up, down, sib):
            send("k", b, to)
            send("v", b, to)

    def hop_far(yy):
        b = block(z2, yy, core)
        arrived("k", b)
        arrived("v", b)
        send("k", b, sib)
        send("v", b, sib)

    hop_own()

    table_load.wait()
    first_row = (ctx * NTP + tp) * VROWS
    lanes = lax.broadcasted_iota(jnp.int32, (64, VROWS), 1)
    picks = (ids[...] - first_row == lanes).astype(jnp.bfloat16)
    for n in range(NTP):
        cols = slice(n * PIECE, (n + 1) * PIECE)
        es[n] = jnp.dot(picks, tab[:, cols], preferred_element_type=jnp.float32).astype(jnp.bfloat16)
    er[tp] = es[tp]

    @pl.loop(1, NTP)
    def _(i):
        to = (tp + i) % NTP
        remote(es.at[to], er.at[tp], e1s.at[i], e1r.at[tp], ctx, to).start()

    light = chip < 4
    moved = jnp.where(light, 4 - chip, chip - 3)
    partner = block(3 - z, 1 - yh, core)
    kept = jnp.where(light, HEADS, HEADS - moved)

    def project_queries(first):
        raw = jnp.dot(x[...], wq[:, first * HD:(first + 4) * HD], preferred_element_type=jnp.float32)
        for h in range(4):
            q[first + h] = rotated(raw[:, h * HD:(h + 1) * HD], q_gain[...], cosine, sine)

    query_loads[0].wait()
    project_queries(4)

    def query_copy(f):
        return remote(q.at[kept + f], q.at[HEADS + f], qs.at[f], qr.at[f], partner, tp)

    @pl.when(jnp.logical_not(light))
    def _():
        @pl.loop(0, moved)
        def _(f):
            query_copy(f).start()

    @pl.loop(1, NTP)
    def _(i):
        frm = (tp + i) % NTP
        remote(es.at[frm], er.at[frm], e1s.at[i], e1r.at[frm], ctx, frm).wait_recv()

    piece = er[0].astype(jnp.float32)
    for n in range(1, NTP):
        piece = piece + er[n].astype(jnp.float32)
    piece = jnp.dot(spread[...], piece.astype(jnp.bfloat16), preferred_element_type=jnp.float32)
    eb[...] = piece.astype(jnp.bfloat16).reshape(NCTX, 16, PIECE)
    ec[ctx] = eb[ctx]

    @pl.loop(1, NCTX)
    def _(i):
        to = (ctx + i) % NCTX
        remote(eb.at[to], ec.at[ctx], e2s.at[i], e2r.at[ctx], to, tp).start()

    query_loads[1].wait()
    project_queries(0)
    hop_ring(yh)

    @pl.loop(1, NCTX)
    def _(i):
        frm = (ctx + i) % NCTX
        remote(eb.at[frm], ec.at[frm], e2s.at[i], e2r.at[frm], frm, tp).wait_recv()

    piece = ec[0].astype(jnp.float32)
    for n in range(1, NCTX):
        piece = piece + ec[n].astype(jnp.float32)
    eh[tp] = piece.astype(jnp.bfloat16)

    def piece_copy(i, to, frm):
        return remote(eh.at[frm], eh.at[frm], e3s.at[i], e3r.at[frm], ctx, to)

    @pl.loop(1, NTP)
    def _(i):
        piece_copy(i, (tp + i) % NTP, tp).start()

    ones = jnp.ones((16, PAIR), jnp.bfloat16)

    def pair_keys(j):
        return kbuf[pl.ds(2 * j, 2)].reshape(PAIR, HD)

    def pair_values(j):
        values = jnp.concatenate([vbuf[2 * j], vbuf[2 * j + 1]], axis=1)
        return jnp.concatenate([values, ones], axis=0)

    def scores(keys, queries):
        return lax.dot_general(keys, queries, (((1,), (1,)), ((), ())), preferred_element_type=jnp.float32)

    def pipeline(units, first, second, third):
        held, mixed = {}, {}
        count = len(units)
        for t in range(count + 2):
            if t < count:
                held[t] = first(units[t])
            if 0 <= t - 2:
                third(units[t - 2], mixed.pop(t - 2))
            if 0 <= t - 1 < count:
                mixed[t - 1] = second(units[t - 1], held.pop(t - 1))

    def unit_scores(unit):
        j, source, _ = unit
        return scores(pair_keys(j), q[source])

    arrived("k", sib)
    arrived("v", sib)
    later = lax.broadcasted_iota(jnp.int32, (PAIR, ROWS), 0) - lax.broadcasted_iota(jnp.int32, (PAIR, ROWS), 1)

    def open_weights(unit, s):
        s = jnp.where(later <= core * ROWS, s, LOW)
        peak = jnp.max(s, axis=0, keepdims=True) * SCALE
        top[unit[2], :1, :] = peak
        return jnp.exp2(s * SCALE - peak).astype(jnp.bfloat16)

    def open_mix(unit, weights):
        acc[unit[2]] = jnp.dot(pair_values(unit[0]), weights, preferred_element_type=jnp.float32)

    def next_weights(unit, s):
        before = top[unit[2], :1, :]
        peak = jnp.maximum(before, jnp.max(s, axis=0, keepdims=True) * SCALE)
        top[unit[2], :1, :] = peak
        return jnp.exp2(s * SCALE - peak).astype(jnp.bfloat16), jnp.exp2(before - peak)

    def next_mix(unit, weights):
        w, factor = weights
        slot = unit[2]
        acc[slot] = acc[slot] * factor + jnp.dot(pair_values(unit[0]), w, preferred_element_type=jnp.float32)

    def open_heads(begin, count, j):
        @pl.loop(0, (count + 3) // 4)
        def _(g):
            units = []
            for n in range(4):
                h = g * 4 + n
                use = h < count
                units.append((j, jnp.where(use, begin + h, 0), jnp.where(use, begin + h, SPARE)))
            pipeline(units, unit_scores, open_weights, open_mix)

    open_heads(0, kept, chip)
    hop_across()
    hop_far(yh)

    @pl.loop(1, NTP)
    def _(i):
        frm = (tp + i) % NTP
        piece_copy(i, frm, frm).wait_recv()

    hidden = jnp.concatenate([eh[n] for n in range(NTP)], axis=1).astype(jnp.float32)
    xs[...] = normed(hidden)
    step_c, step_s = far_c[NCTX:NCTX + 1, :], far_s[NCTX:NCTX + 1, :]
    dec_c = near_c[:16, :] * step_c - near_s[:16, :] * step_s
    dec_s = near_s[:16, :] * step_c + near_c[:16, :] * step_s
    step_kv = jnp.dot(xs[...], wkv[...], preferred_element_type=jnp.float32)
    step_k = rotated(step_kv[:, :HD], k_gain[...], dec_c, dec_s)
    step_v = step_kv[:, HD:].astype(jnp.bfloat16)
    for g in range(2):
        raw = jnp.dot(xs[...], wq[:, g * 512:(g + 1) * 512], preferred_element_type=jnp.float32)
        for h in range(4):
            rows = slice((g * 4 + h) * 16, (g * 4 + h + 1) * 16)
            qd[rows, :] = rotated(raw[:, h * HD:(h + 1) * HD], q_gain[...], dec_c, dec_s)

    own = scores(step_k, qd[...])
    step = lax.broadcasted_iota(jnp.int32, (16, HD), 1) % 16
    own = jnp.where(lax.broadcasted_iota(jnp.int32, (16, HD), 0) <= step, own, LOW)
    peak = jnp.max(own, axis=0, keepdims=True) * SCALE
    weights = jnp.exp2(own * SCALE - peak).astype(jnp.bfloat16)
    topd[:1, :] = peak
    step_values = jnp.concatenate([step_v, jnp.ones((16, 16), jnp.bfloat16)], axis=1)
    accd[...] = lax.dot_general(
        step_values, weights, (((0,), (0,)), ((), ())), preferred_element_type=jnp.float32
    )

    hop_ring(1 - yh)
    hop_far(1 - yh)
    for zz, yy in ((zm, yh), (zp, yh), (z2, yh), (z, 1 - yh), (zm, 1 - yh), (zp, 1 - yh), (z2, 1 - yh)):
        arrived("k", block(zz, yy, 1 - core))
        arrived("v", block(zz, yy, 1 - core))

    @pl.when(light)
    def _():
        @pl.loop(0, moved)
        def _(f):
            query_copy(f).wait_recv()

        open_heads(HEADS, moved, 7 - chip)

    own_units = kept * chip
    all_units = jnp.where(light, own_units + moved * (7 - chip), own_units)
    top[SPARE] = jnp.zeros((8, ROWS), jnp.float32)

    @pl.loop(0, (all_units + GROUP - 1) // GROUP)
    def _(g):
        units = []
        for n in range(GROUP):
            u = g * GROUP + n
            rest = u - own_units
            mine = rest < 0
            use = u < all_units
            j = jnp.where(mine, u // kept, rest // moved)
            slot = jnp.where(mine, u % kept, HEADS + rest % moved)
            units.append((jnp.where(use, j, 0), jnp.where(use, slot, 0), jnp.where(use, slot, SPARE)))
        pipeline(units, unit_scores, next_weights, next_mix)

    def finished(slot):
        mix = acc[slot]
        return (mix[:HD] * (1.0 / mix[HD:HD + 1])).T.astype(jnp.bfloat16)

    def result_copy(f):
        return remote(fsend.at[f], frecv.at[f], fs.at[f], fr.at[f], partner, tp)

    @pl.when(light)
    def _():
        @pl.loop(0, moved)
        def _(f):
            fsend[f] = finished(HEADS + f)
            result_copy(f).start()

    def step_weights(j, s):
        before = topd[:1, :]
        peak = jnp.maximum(before, jnp.max(s, axis=0, keepdims=True) * SCALE)
        topd[:1, :] = peak
        return jnp.exp2(s * SCALE - peak).astype(jnp.bfloat16), jnp.exp2(before - peak)

    def step_mix(j, weights):
        w, factor = weights
        accd[...] = accd[...] * factor + jnp.dot(pair_values(j), w, preferred_element_type=jnp.float32)

    @pl.loop(0, 2)
    def _(g):
        pipeline([g * 4 + n for n in range(4)], lambda j: scores(pair_keys(j), qd[...]), step_weights, step_mix)

    mix = accd[...]
    steps = (mix[:HD] * (1.0 / mix[HD:HD + 1])).T.astype(jnp.bfloat16)
    for h in range(HEADS):
        dec[:, h * HD:(h + 1) * HD] = steps[h * 16:(h + 1) * 16, :]

    @pl.loop(0, kept)
    def _(h):
        out[:, pl.ds(pl.multiple_of(h * HD, HD), HD)] = finished(h)

    @pl.when(jnp.logical_not(light))
    def _():
        @pl.loop(0, moved)
        def _(f):
            result_copy(f).wait_recv()
            out[:, pl.ds(pl.multiple_of((kept + f) * HD, HD), HD)] = frecv[f]
            query_copy(f).wait_send()

    @pl.when(light)
    def _():
        @pl.loop(0, moved)
        def _(f):
            result_copy(f).wait_send()

    for _, copy in sent:
        copy.wait_send()

    @pl.loop(1, NTP)
    def _(i):
        to = (tp + i) % NTP
        remote(es.at[to], er.at[tp], e1s.at[i], e1r.at[tp], ctx, to).wait_send()
        piece_copy(i, to, tp).wait_send()

    @pl.loop(1, NCTX)
    def _(i):
        to = (ctx + i) % NCTX
        remote(eb.at[to], ec.at[ctx], e2s.at[i], e2r.at[ctx], to, tp).wait_send()


def body(prompt, norm_gain, w_query, w_key, w_value, query_gain, key_gain, table, sampled):
    near_c, near_s, far_c, far_s = rope_tables(NCTX * ROWS)
    spread = np.zeros((NCTX * 16, 64), np.float32)
    for s in range(NCTX):
        for j in range(4):
            spread[s * 16 + j, s * 4 + j] = 1.0
    hbm = pl.BlockSpec(memory_space=pl.ANY)
    vmem = pl.BlockSpec(memory_space=pltpu.VMEM)
    bf, f32 = jnp.bfloat16, jnp.float32
    dma = pltpu.SemaphoreType.DMA
    out, dec = pl.pallas_call(
        kernel,
        out_shape=(
            jax.ShapeDtypeStruct((ROWS, HEADS * HD), bf),
            jax.ShapeDtypeStruct((16, HEADS * HD), bf),
        ),
        in_specs=[hbm, vmem, hbm, hbm, hbm, vmem, vmem, hbm] + [vmem] * 6,
        out_specs=(vmem, vmem),
        scratch_shapes=[
            pltpu.VMEM((ROWS, D), bf),
            pltpu.VMEM((D, HEADS * HD), bf),
            pltpu.VMEM((D, 2 * HD), bf),
            pltpu.VMEM((VROWS, D), bf),
            pltpu.VMEM((12, ROWS, HD), bf),
            pltpu.VMEM((NCTX, ROWS, HD), bf),
            pltpu.VMEM((NCTX, HD, ROWS), bf),
            pltpu.VMEM((SPARE + 1, ACC, ROWS), f32),
            pltpu.VMEM((SPARE + 1, 8, ROWS), f32),
            pltpu.VMEM((NTP, 64, PIECE), bf),
            pltpu.VMEM((NTP, 64, PIECE), bf),
            pltpu.VMEM((NCTX, 16, PIECE), bf),
            pltpu.VMEM((NCTX, 16, PIECE), bf),
            pltpu.VMEM((NTP, 16, PIECE), bf),
            pltpu.VMEM((16, D), bf),
            pltpu.VMEM((HD, HD), bf),
            pltpu.VMEM((ACC, HD), f32),
            pltpu.VMEM((8, HD), f32),
            pltpu.VMEM((4, ROWS, HD), bf),
            pltpu.VMEM((4, ROWS, HD), bf),
            dma((7,)), dma((2,)),
            dma((15,)), dma((NCTX,)), dma((15,)), dma((NCTX,)),
            dma((NTP,)), dma((NTP,)), dma((NCTX,)), dma((NCTX,)), dma((NTP,)), dma((NTP,)),
            dma((4,)), dma((4,)), dma((4,)), dma((4,)),
        ],
        compiler_params=pltpu.CompilerParams(
            collective_id=0, has_side_effects=True, vmem_limit_bytes=62 * 2**20
        ),
    )(
        prompt, norm_gain[None, :], w_query, w_key, w_value, query_gain[None, :], key_gain[None, :], table,
        sampled.reshape(64, 1), near_c, near_s, far_c, far_s, spread.astype(jnp.bfloat16),
    )
    return out, dec[None, :4]


def solution(mesh):
    in_specs = (
        P("ctx", None),
        P(),
        P(None, "tp"),
        P(None, "tp"),
        P(None, "tp"),
        P(),
        P(),
        P(("ctx", "tp"), None),
        P(),
    )
    out_specs = (P("ctx", "tp"), P("ctx", None, "tp"))
    return jax.shard_map(body, mesh=mesh, in_specs=in_specs, out_specs=out_specs, check_vma=False)
```

```python
import functools

import jax
import jax.numpy as jnp
import numpy as np
from jax import lax
from jax.experimental import pallas as pl
from jax.experimental.pallas import tpu as pltpu
from jax.sharding import PartitionSpec as P

MESH = pl.DeviceIdType.MESH
EPS = 1e-06
THETA = 1000000.0
HD = 128
ROWS = 512
D = 5120
PAIR = 2 * ROWS
HEADS = 8
NCTX = 16
NTP = 8
VROWS = 608
PIECE = D // NTP
SCALE = HD ** (-0.5) * 1.4426950408889634
LOW = -1e30
GROUP = 5
SPARE = 11
TAKEN = (3, 3, 2, 1)
ACC = HD + 16


def rope_tables(prompt_len):
    half = HD // 2
    freqs = THETA ** (-np.arange(half, dtype=np.float64) / half)
    freqs = np.concatenate([freqs, freqs])[None, :]
    sign = np.concatenate([-np.ones(half), np.ones(half)])[None, :]
    near = np.arange(ROWS, dtype=np.float64)[:, None] * freqs
    far = (np.arange(prompt_len // ROWS + 1, dtype=np.float64) * ROWS)[:, None] * freqs
    tables = (np.cos(near), np.sin(near) * sign, np.cos(far), np.sin(far) * sign)
    return [t.astype(np.float32) for t in tables]


def pair_lists(chip):
    zz, yy = chip // 2, chip % 2
    at = lambda dz, y: (zz + dz) % 4 * 2 + y
    soon = [at(0, 1 - yy), at(3, yy), at(1, yy), at(2, yy)]
    late = [at(3, 1 - yy), at(1, 1 - yy), at(2, 1 - yy)]
    cut = lambda pairs, limit: [j for j in pairs if j < limit]
    lists = [cut(soon, chip), cut(late, chip)]
    lists += [cut([chip] + soon, 7 - chip), cut(late, 7 - chip)] if chip < 4 else [[], []]
    return [(len(pairs), sum(j << (3 * k) for k, j in enumerate(pairs))) for pairs in lists]


PAIR_LISTS = [pair_lists(chip) for chip in range(8)]


def pick(index, values):
    result = index * 0 + values[-1]
    for n, value in enumerate(values[:-1]):
        result = result + (index == n).astype(jnp.int32) * (value - values[-1])
    return result


def kernel(
    prompt, gain, w_query, w_key, w_value, q_gain, k_gain, table, ids, near_c, near_s, far_c, far_s, spread,
    out, dec,
    x, wq, wkv, tab, q, kbuf, vbuf, acc, top, es, er, eb, ec, eh, xs, qd, accd, topd, fsend, frecv,
    load_sem, wq_sem, ks, kr, vs, vr, e1s, e1r, e2s, e2r, e3s, e3r, qs, qr, fs, fr,
):
    ctx = lax.axis_index("ctx")
    tp = lax.axis_index("tp")
    chip = ctx // 2
    core = ctx % 2
    z = ctx // 4
    yh = chip % 2

    def remote(src, dst, send, recv, to_ctx, to_tp):
        return pltpu.make_async_remote_copy(
            src_ref=src, dst_ref=dst, send_sem=send, recv_sem=recv,
            device_id=(to_ctx, to_tp), device_id_type=MESH,
        )

    prompt_loads = []
    for n in range(4):
        rows = pl.ds(n * 128, 128)
        prompt_loads.append(pltpu.make_async_copy(prompt.at[rows], x.at[rows], load_sem.at[n]))
    key_load = pltpu.make_async_copy(w_key, wkv.at[:, pl.ds(0, HD)], load_sem.at[4])
    value_load = pltpu.make_async_copy(w_value, wkv.at[:, pl.ds(HD, HD)], load_sem.at[5])
    table_load = pltpu.make_async_copy(table, tab, load_sem.at[6])
    query_loads = []
    for n in range(2):
        cols = pl.ds((1 - n) * 512, 512)
        query_loads.append(pltpu.make_async_copy(w_query.at[:, cols], wq.at[:, cols], wq_sem.at[n]))
    for load in (*prompt_loads, key_load, value_load):
        load.start()

    barrier = pltpu.get_barrier_semaphore()

    @pl.loop(1, NCTX)
    def _(i):
        pl.semaphore_signal(barrier, inc=1, device_id=((ctx + i) % NCTX, tp), device_id_type=MESH)

    @pl.loop(1, NTP)
    def _(i):
        pl.semaphore_signal(barrier, inc=1, device_id=(ctx, (tp + i) % NTP), device_id_type=MESH)

    def normed(rows_f32):
        mean_square = jnp.mean(rows_f32 * rows_f32, axis=-1, keepdims=True)
        return (rows_f32 * lax.rsqrt(mean_square + EPS) * gain[...]).astype(jnp.bfloat16)

    for n in range(4):
        prompt_loads[n].wait()

        @pl.loop(0, 8, unroll=2)
        def _(i):
            rows = pl.ds(pl.multiple_of(n * 128 + i * 16, 16), 16)
            x[rows, :] = normed(x[rows, :].astype(jnp.float32))

        if n == 2:
            query_loads[0].start()
    query_loads[1].start()
    table_load.start()

    def rotated(raw, head_gain, cosine, sine):
        mean_square = jnp.mean(raw * raw, axis=-1, keepdims=True)
        y = raw * lax.rsqrt(mean_square + EPS) * head_gain
        return (y * cosine + pltpu.roll(y, HD // 2, 1) * sine).astype(jnp.bfloat16)

    base_c, base_s = far_c[pl.ds(ctx, 1), :], far_s[pl.ds(ctx, 1), :]
    cosine = near_c[...] * base_c - near_s[...] * base_s
    sine = near_s[...] * base_c + near_c[...] * base_s

    key_load.wait()
    value_load.wait()
    kv = jnp.dot(x[...], wkv[...], preferred_element_type=jnp.float32)
    kbuf[ctx] = rotated(kv[:, :HD], k_gain[...], cosine, sine)
    vbuf[ctx] = kv[:, HD:].T.astype(jnp.bfloat16)

    pl.semaphore_wait(barrier, NCTX + NTP - 2)

    def block(zz, yy, cc):
        return zz * 4 + yy * 2 + cc

    zp, zm, z2 = (z + 1) % 4, (z + 3) % 4, (z + 2) % 4
    sib = block(z, yh, 1 - core)
    up, down, across = block(zp, yh, core), block(zm, yh, core), block(z, 1 - yh, core)
    late_left, late_right, late_far = (block(n, 1 - yh, core) for n in (zm, zp, z2))
    sent = []

    def block_copy(kind, n, b, to):
        buffer, out_sem, in_sem = (kbuf, ks, kr) if kind == "k" else (vbuf, vs, vr)
        return remote(buffer.at[b], buffer.at[b], out_sem.at[n], in_sem.at[b], to, tp)

    def send(kind, b, to):
        n = sum(1 for item in sent if item[0] == kind)
        block_copy(kind, n, b, to).start()
        sent.append((kind, n, b, to))

    def arrived(kind, b):
        block_copy(kind, 0, b, sib).wait_recv()

    def hop_own():
        send("k", ctx, up)
        send("v", ctx, down)
        send("k", ctx, across)
        send("v", ctx, across)
        send("v", ctx, up)
        send("k", ctx, down)
        send("k", ctx, sib)
        send("v", ctx, sib)

    def hop_ring():
        left, right = block(zm, yh, core), block(zp, yh, core)
        arrived("k", left)
        send("k", left, up)
        arrived("v", right)
        send("v", right, down)
        arrived("v", left)
        arrived("k", right)
        for b in (left, right):
            send("k", b, sib)
            send("v", b, sib)

    def hop_across():
        arrived("k", across)
        arrived("v", across)
        for to in (up, down, sib):
            send("k", across, to)
            send("v", across, to)

    def hop_last(b, *more):
        arrived("k", b)
        arrived("v", b)
        for to in (*more, sib):
            send("k", b, to)
            send("v", b, to)

    def from_sib(zz, yy):
        arrived("k", block(zz, yy, 1 - core))
        arrived("v", block(zz, yy, 1 - core))

    hop_own()

    light = chip < 4
    moved = pick(chip, TAKEN + TAKEN[::-1])
    partner = block(3 - z, 1 - yh, core)
    kept = jnp.where(light, HEADS, HEADS - moved)

    def project_queries(first):
        raw = jnp.dot(x[...], wq[:, first * HD:(first + 4) * HD], preferred_element_type=jnp.float32)
        for h in range(4):
            q[first + h] = rotated(raw[:, h * HD:(h + 1) * HD], q_gain[...], cosine, sine)

    query_loads[0].wait()
    project_queries(4)

    def query_copy(f):
        return remote(q.at[kept + f], q.at[HEADS + f], qs.at[f], qr.at[f], partner, tp)

    @pl.when(jnp.logical_not(light))
    def _():
        @pl.loop(0, moved)
        def _(f):
            query_copy(f).start()

    query_loads[1].wait()
    project_queries(0)
    table_load.wait()
    first_row = (ctx * NTP + tp) * VROWS
    lanes = (lax.broadcasted_iota(jnp.int32, (16, VROWS), 1) + first_row).astype(jnp.float32)
    diagonal = lax.broadcasted_iota(jnp.int32, (16, 16), 0) == lax.broadcasted_iota(jnp.int32, (16, 16), 1)
    picks = []
    for j in range(4):
        wanted = jnp.where(diagonal, ids[j:j + 1, :].astype(jnp.float32), 0.0)
        picks.append((jnp.sum(wanted, axis=1, keepdims=True) == lanes).astype(jnp.float32))
    picks = jnp.concatenate(picks, axis=0).astype(jnp.bfloat16)
    for n in range(NTP):
        cols = slice(n * PIECE, (n + 1) * PIECE)
        es[n] = jnp.dot(picks, tab[:, cols], preferred_element_type=jnp.float32).astype(jnp.bfloat16)
    er[tp] = es[tp]

    @pl.loop(1, NTP)
    def _(i):
        to = (tp + i) % NTP
        remote(es.at[to], er.at[tp], e1s.at[i], e1r.at[tp], ctx, to).start()

    ones = jnp.ones((16, PAIR), jnp.bfloat16)

    def pair_keys(j):
        return kbuf[pl.ds(2 * j, 2)].reshape(PAIR, HD)

    def pair_values(j):
        values = jnp.concatenate([vbuf[2 * j], vbuf[2 * j + 1]], axis=1)
        return jnp.concatenate([values, ones], axis=0)

    def scores(keys, queries):
        return lax.dot_general(keys, queries, (((1,), (1,)), ((), ())), preferred_element_type=jnp.float32)

    def pipeline(units, first, second, third):
        held, mixed = {}, {}
        count = len(units)
        for t in range(count + 2):
            if t < count:
                held[t] = first(units[t])
            if 0 <= t - 2:
                third(units[t - 2], mixed.pop(t - 2))
            if 0 <= t - 1 < count:
                mixed[t - 1] = second(units[t - 1], held.pop(t - 1))

    def unit_scores(unit):
        j, source, _ = unit
        return scores(pair_keys(j), q[source])

    arrived("k", sib)
    arrived("v", sib)
    later = lax.broadcasted_iota(jnp.int32, (PAIR, ROWS), 0) - lax.broadcasted_iota(jnp.int32, (PAIR, ROWS), 1)

    def open_weights(unit, s):
        s = jnp.where(later <= core * ROWS, s, LOW)
        peak = jnp.max(s, axis=0, keepdims=True) * SCALE
        top[unit[2], :1, :] = peak
        return jnp.exp2(s * SCALE - peak).astype(jnp.bfloat16)

    def open_mix(unit, weights):
        acc[unit[2]] = jnp.dot(pair_values(unit[0]), weights, preferred_element_type=jnp.float32)

    def next_weights(unit, s):
        before = top[unit[2], :1, :]
        peak = jnp.maximum(before, jnp.max(s, axis=0, keepdims=True) * SCALE)
        top[unit[2], :1, :] = peak
        return jnp.exp2(s * SCALE - peak).astype(jnp.bfloat16), jnp.exp2(before - peak)

    def last_weights(unit, s):
        return next_weights(unit, jnp.where(later <= core * ROWS, s, LOW))

    def next_mix(unit, weights):
        w, factor = weights
        slot = unit[2]
        acc[slot] = acc[slot] * factor + jnp.dot(pair_values(unit[0]), w, preferred_element_type=jnp.float32)

    def open_heads(begin, count):
        units = []
        for n in range(4):
            use = n < count
            units.append((chip, jnp.where(use, begin + n, 0), jnp.where(use, begin + n, SPARE)))
        pipeline(units, unit_scores, open_weights, open_mix)

    open_heads(chip * 0, chip * 0 + 4)
    hop_ring()
    open_heads(chip * 0 + 4, kept - 4)
    hop_across()
    @pl.loop(1, NTP)
    def _(i):
        frm = (tp + i) % NTP
        remote(es.at[frm], er.at[frm], e1s.at[i], e1r.at[frm], ctx, frm).wait_recv()

    piece = er[0].astype(jnp.float32)
    for n in range(1, NTP):
        piece = piece + er[n].astype(jnp.float32)
    piece = jnp.dot(spread[...], piece.astype(jnp.bfloat16), preferred_element_type=jnp.float32)
    eb[...] = piece.astype(jnp.bfloat16).reshape(NCTX, 16, PIECE)
    ec[ctx] = eb[ctx]

    @pl.loop(1, NCTX)
    def _(i):
        to = (ctx + i) % NCTX
        remote(eb.at[to], ec.at[ctx], e2s.at[i], e2r.at[ctx], to, tp).start()

    hop_last(block(z2, yh, core), across)
    for zz, yy in ((z, 1 - yh), (zm, yh), (zp, yh), (z2, yh)):
        from_sib(zz, yy)

    @pl.when(light)
    def _():
        @pl.loop(0, moved)
        def _(f):
            query_copy(f).wait_recv()
            acc[HEADS + f] = jnp.zeros((ACC, ROWS), jnp.float32)
            top[HEADS + f] = jnp.full((8, ROWS), LOW, jnp.float32)

    acc[SPARE] = jnp.zeros((ACC, ROWS), jnp.float32)
    top[SPARE] = jnp.zeros((8, ROWS), jnp.float32)

    def settle(turn, k, h, sizes):
        for n in range(2):
            end = (turn == n) & (k >= sizes[n])
            turn = jnp.where(end, n + 1, turn)
            k = jnp.where(end, 0, k)
        return turn, k, h

    def run_pairs(own_list, other_list, own_first, between=None):
        tables = [[PAIR_LISTS[c][n] for c in range(8)] for n in (own_list, other_list)]
        sizes = [pick(chip, [entry[0] for entry in t]) for t in tables]
        codes = [pick(chip, [entry[1] for entry in t]) for t in tables]
        widths, bases = [kept, moved], [chip * 0, chip * 0 + HEADS]
        if not own_first:
            for items in (sizes, codes, widths, bases):
                items.reverse()
        total = sizes[0] * widths[0] + sizes[1] * widths[1]

        def step(g, state):
            if between is not None:
                between(g)
            units = []
            for n in range(GROUP):
                turn, k, h = state
                first = turn == 0
                use = turn < 2
                j = lax.shift_right_logical(jnp.where(first, codes[0], codes[1]), 3 * k) % 8
                slot = jnp.where(first, bases[0], bases[1]) + h
                units.append((jnp.where(use, j, chip), jnp.where(use, slot, 0), jnp.where(use, slot, SPARE)))
                h = h + 1
                wrap = h >= jnp.where(first, widths[0], widths[1])
                state = settle(turn, k + wrap.astype(jnp.int32), jnp.where(wrap, 0, h), sizes)
            pipeline(units, unit_scores, next_weights, next_mix)
            return state

        start = settle(chip * 0, chip * 0, chip * 0, sizes)
        lax.fori_loop(0, (total + GROUP - 1) // GROUP, step, start)

    def hops_between(g):
        @pl.when(g == 1)
        def _():
            hop_last(late_left)
            hop_last(late_right)

        @pl.when(g == 2)
        def _():
            hop_last(late_far)

    run_pairs(0, 2, True, hops_between)

    @pl.loop(1, NCTX)
    def _(i):
        frm = (ctx + i) % NCTX
        remote(eb.at[frm], ec.at[frm], e2s.at[i], e2r.at[frm], frm, tp).wait_recv()

    piece = ec[0].astype(jnp.float32)
    for n in range(1, NCTX):
        piece = piece + ec[n].astype(jnp.float32)
    eh[tp] = piece.astype(jnp.bfloat16)

    def piece_copy(i, to, frm):
        return remote(eh.at[frm], eh.at[frm], e3s.at[i], e3r.at[frm], ctx, to)

    @pl.loop(1, NTP)
    def _(i):
        piece_copy(i, (tp + i) % NTP, tp).start()

    for zz in (zm, zp, z2):
        from_sib(zz, 1 - yh)
    run_pairs(1, 3, False)

    def finished(slot):
        mix = acc[slot]
        return (mix[:HD] * (1.0 / mix[HD:HD + 1])).T.astype(jnp.bfloat16)

    def result_copy(f):
        return remote(fsend.at[f], frecv.at[f], fs.at[f], fr.at[f], partner, tp)

    @pl.when(light)
    def _():
        units = []
        for f in range(3):
            use = f < moved
            slot = HEADS + f + 0 * chip
            units.append((7 - chip, jnp.where(use, slot, 0), jnp.where(use, slot, SPARE)))
        pipeline(units, unit_scores, last_weights, next_mix)

        @pl.loop(0, moved)
        def _(f):
            fsend[f] = finished(HEADS + f)
            result_copy(f).start()

    @pl.loop(1, NTP)
    def _(i):
        frm = (tp + i) % NTP
        piece_copy(i, frm, frm).wait_recv()

    hidden = jnp.concatenate([eh[n] for n in range(NTP)], axis=1).astype(jnp.float32)
    xs[...] = normed(hidden)
    step_c, step_s = far_c[NCTX:NCTX + 1, :], far_s[NCTX:NCTX + 1, :]
    dec_c = near_c[:16, :] * step_c - near_s[:16, :] * step_s
    dec_s = near_s[:16, :] * step_c + near_c[:16, :] * step_s
    step_kv = jnp.dot(xs[...], wkv[...], preferred_element_type=jnp.float32)
    step_k = rotated(step_kv[:, :HD], k_gain[...], dec_c, dec_s)
    step_v = step_kv[:, HD:].astype(jnp.bfloat16)
    for g in range(2):
        raw = jnp.dot(xs[...], wq[:, g * 512:(g + 1) * 512], preferred_element_type=jnp.float32)
        for h in range(4):
            rows = slice((g * 4 + h) * 16, (g * 4 + h + 1) * 16)
            qd[rows, :] = rotated(raw[:, h * HD:(h + 1) * HD], q_gain[...], dec_c, dec_s)

    own = scores(step_k, qd[...])
    step = lax.broadcasted_iota(jnp.int32, (16, HD), 1) % 16
    own = jnp.where(lax.broadcasted_iota(jnp.int32, (16, HD), 0) <= step, own, LOW)
    peak = jnp.max(own, axis=0, keepdims=True) * SCALE
    weights = jnp.exp2(own * SCALE - peak).astype(jnp.bfloat16)
    topd[:1, :] = peak
    step_values = jnp.concatenate([step_v, jnp.ones((16, 16), jnp.bfloat16)], axis=1)
    accd[...] = lax.dot_general(
        step_values, weights, (((0,), (0,)), ((), ())), preferred_element_type=jnp.float32
    )

    def step_weights(j, s):
        before = topd[:1, :]
        peak = jnp.maximum(before, jnp.max(s, axis=0, keepdims=True) * SCALE)
        topd[:1, :] = peak
        return jnp.exp2(s * SCALE - peak).astype(jnp.bfloat16), jnp.exp2(before - peak)

    def step_mix(j, weights):
        w, factor = weights
        accd[...] = accd[...] * factor + jnp.dot(pair_values(j), w, preferred_element_type=jnp.float32)

    @pl.loop(0, 2)
    def _(g):
        pipeline([g * 4 + n for n in range(4)], lambda j: scores(pair_keys(j), qd[...]), step_weights, step_mix)

    mix = accd[...]
    steps = (mix[:HD] * (1.0 / mix[HD:HD + 1])).T.astype(jnp.bfloat16)
    for h in range(HEADS):
        dec[:, h * HD:(h + 1) * HD] = steps[h * 16:(h + 1) * 16, :]

    @pl.loop(0, kept)
    def _(h):
        out[:, pl.ds(pl.multiple_of(h * HD, HD), HD)] = finished(h)

    @pl.when(jnp.logical_not(light))
    def _():
        @pl.loop(0, moved)
        def _(f):
            result_copy(f).wait_recv()
            out[:, pl.ds(pl.multiple_of((kept + f) * HD, HD), HD)] = frecv[f]
            query_copy(f).wait_send()

    @pl.when(light)
    def _():
        @pl.loop(0, moved)
        def _(f):
            result_copy(f).wait_send()

    for item in sent:
        block_copy(*item).wait_send()

    @pl.loop(1, NTP)
    def _(i):
        to = (tp + i) % NTP
        remote(es.at[to], er.at[tp], e1s.at[i], e1r.at[tp], ctx, to).wait_send()
        piece_copy(i, to, tp).wait_send()

    @pl.loop(1, NCTX)
    def _(i):
        to = (ctx + i) % NCTX
        remote(eb.at[to], ec.at[ctx], e2s.at[i], e2r.at[ctx], to, tp).wait_send()


def body(prompt, norm_gain, w_query, w_key, w_value, query_gain, key_gain, table, sampled):
    near_c, near_s, far_c, far_s = rope_tables(NCTX * ROWS)
    spread = np.zeros((NCTX * 16, 64), np.float32)
    for s in range(NCTX):
        for j in range(4):
            spread[s * 16 + j, j * 16 + s] = 1.0
    hbm = pl.BlockSpec(memory_space=pl.ANY)
    vmem = pl.BlockSpec(memory_space=pltpu.VMEM)
    bf, f32 = jnp.bfloat16, jnp.float32
    dma = pltpu.SemaphoreType.DMA
    out, dec = pl.pallas_call(
        kernel,
        out_shape=(
            jax.ShapeDtypeStruct((ROWS, HEADS * HD), bf),
            jax.ShapeDtypeStruct((16, HEADS * HD), bf),
        ),
        in_specs=[hbm, vmem, hbm, hbm, hbm, vmem, vmem, hbm] + [vmem] * 6,
        out_specs=(vmem, vmem),
        scratch_shapes=[
            pltpu.VMEM((ROWS, D), bf),
            pltpu.VMEM((D, HEADS * HD), bf),
            pltpu.VMEM((D, 2 * HD), bf),
            pltpu.VMEM((VROWS, D), bf),
            pltpu.VMEM((12, ROWS, HD), bf),
            pltpu.VMEM((NCTX, ROWS, HD), bf),
            pltpu.VMEM((NCTX, HD, ROWS), bf),
            pltpu.VMEM((SPARE + 1, ACC, ROWS), f32),
            pltpu.VMEM((SPARE + 1, 8, ROWS), f32),
            pltpu.VMEM((NTP, 64, PIECE), bf),
            pltpu.VMEM((NTP, 64, PIECE), bf),
            pltpu.VMEM((NCTX, 16, PIECE), bf),
            pltpu.VMEM((NCTX, 16, PIECE), bf),
            pltpu.VMEM((NTP, 16, PIECE), bf),
            pltpu.VMEM((16, D), bf),
            pltpu.VMEM((HD, HD), bf),
            pltpu.VMEM((ACC, HD), f32),
            pltpu.VMEM((8, HD), f32),
            pltpu.VMEM((4, ROWS, HD), bf),
            pltpu.VMEM((4, ROWS, HD), bf),
            dma((7,)), dma((2,)),
            dma((16,)), dma((NCTX,)), dma((16,)), dma((NCTX,)),
            dma((NTP,)), dma((NTP,)), dma((NCTX,)), dma((NCTX,)), dma((NTP,)), dma((NTP,)),
            dma((4,)), dma((4,)), dma((4,)), dma((4,)),
        ],
        compiler_params=pltpu.CompilerParams(
            collective_id=0, has_side_effects=True, vmem_limit_bytes=62 * 2**20
        ),
    )(
        prompt, norm_gain[None, :], w_query, w_key, w_value, query_gain[None, :], key_gain[None, :], table,
        sampled.T, near_c, near_s, far_c, far_s, spread.astype(jnp.bfloat16),
    )
    return out, dec[None, :4]


def solution(mesh):
    in_specs = (
        P("ctx", None),
        P(),
        P(None, "tp"),
        P(None, "tp"),
        P(None, "tp"),
        P(),
        P(),
        P(("ctx", "tp"), None),
        P(),
    )
    out_specs = (P("ctx", "tp"), P("ctx", None, "tp"))
    return jax.shard_map(body, mesh=mesh, in_specs=in_specs, out_specs=out_specs, check_vma=False)
```

```python
import functools

import jax
import jax.numpy as jnp
import numpy as np
from jax import lax
from jax.experimental import pallas as pl
from jax.experimental.pallas import tpu as pltpu
from jax.sharding import PartitionSpec as P

MESH = pl.DeviceIdType.MESH
EPS = 1e-06
THETA = 1000000.0
HD = 128
ROWS = 512
D = 5120
PAIR = 2 * ROWS
HEADS = 8
NCTX = 16
NTP = 8
VROWS = 608
PIECE = D // NTP
SCALE = HD ** (-0.5) * 1.4426950408889634
LOW = -1e30
GROUP = 5
SPARE = 11
TAKEN = (3, 3, 2, 1, 2, 1, 3, 3)
ACC = HD + 16


def rope_tables(prompt_len):
    half = HD // 2
    freqs = THETA ** (-np.arange(half, dtype=np.float64) / half)
    freqs = np.concatenate([freqs, freqs])[None, :]
    sign = np.concatenate([-np.ones(half), np.ones(half)])[None, :]
    near = np.arange(ROWS, dtype=np.float64)[:, None] * freqs
    far = (np.arange(prompt_len // ROWS + 1, dtype=np.float64) * ROWS)[:, None] * freqs
    tables = (np.cos(near), np.sin(near) * sign, np.cos(far), np.sin(far) * sign)
    return [t.astype(np.float32) for t in tables]


def pair_lists(chip):
    zz, yy = chip // 2, chip % 2
    at = lambda dz, y: (zz + dz) % 4 * 2 + y
    soon = [at(0, 1 - yy), at(3, yy), at(1, yy), at(2, yy)]
    late = [at(3, 1 - yy), at(1, 1 - yy), at(2, 1 - yy)]
    cut = lambda pairs, limit: [j for j in pairs if j < limit]
    other = (3 - zz) * 2 + yy if chip < 4 else -1
    lists = [cut(soon, chip), cut([chip] + soon, other), cut(late, other), cut(late, chip)]
    return [(len(pairs), sum(j << (3 * k) for k, j in enumerate(pairs))) for pairs in lists]


PAIR_LISTS = [pair_lists(chip) for chip in range(8)]


def pick(index, values):
    result = index * 0 + values[-1]
    for n, value in enumerate(values[:-1]):
        result = result + (index == n).astype(jnp.int32) * (value - values[-1])
    return result


def kernel(
    prompt, gain, w_query, w_key, w_value, q_gain, k_gain, table, ids, near_c, near_s, far_c, far_s, spread,
    out, dec,
    x, wq, wkv, tab, q, kbuf, vbuf, acc, top, es, e0, er, eb, ec, eh, xs, qd, accd, topd, fsend, frecv,
    load_sem, wq_sem, ks, kr, vs, vr, e0r, e1s, e1r, e2s, e2r, e3s, e3r, qs, qr, fs, fr,
):
    ctx = lax.axis_index("ctx")
    tp = lax.axis_index("tp")
    chip = ctx // 2
    core = ctx % 2
    z = ctx // 4
    yh = chip % 2

    def remote(src, dst, send, recv, to_ctx, to_tp):
        return pltpu.make_async_remote_copy(
            src_ref=src, dst_ref=dst, send_sem=send, recv_sem=recv,
            device_id=(to_ctx, to_tp), device_id_type=MESH,
        )

    prompt_loads = []
    for n in range(4):
        rows = pl.ds(n * 128, 128)
        prompt_loads.append(pltpu.make_async_copy(prompt.at[rows], x.at[rows], load_sem.at[n]))
    key_load = pltpu.make_async_copy(w_key, wkv.at[:, pl.ds(0, HD)], load_sem.at[4])
    value_load = pltpu.make_async_copy(w_value, wkv.at[:, pl.ds(HD, HD)], load_sem.at[5])
    table_load = pltpu.make_async_copy(table, tab, load_sem.at[6])
    query_loads = []
    for n in range(2):
        cols = pl.ds((1 - n) * 512, 512)
        query_loads.append(pltpu.make_async_copy(w_query.at[:, cols], wq.at[:, cols], wq_sem.at[n]))
    for load in (*prompt_loads, key_load, value_load):
        load.start()

    barrier = pltpu.get_barrier_semaphore()

    @pl.loop(1, NCTX)
    def _(i):
        pl.semaphore_signal(barrier, inc=1, device_id=((ctx + i) % NCTX, tp), device_id_type=MESH)

    @pl.loop(1, NTP)
    def _(i):
        pl.semaphore_signal(barrier, inc=1, device_id=(ctx, (tp + i) % NTP), device_id_type=MESH)

    def normed(rows_f32):
        mean_square = jnp.mean(rows_f32 * rows_f32, axis=-1, keepdims=True)
        return (rows_f32 * lax.rsqrt(mean_square + EPS) * gain[...]).astype(jnp.bfloat16)

    for n in range(4):
        prompt_loads[n].wait()

        @pl.loop(0, 8, unroll=2)
        def _(i):
            rows = pl.ds(pl.multiple_of(n * 128 + i * 16, 16), 16)
            x[rows, :] = normed(x[rows, :].astype(jnp.float32))

        if n == 2:
            query_loads[0].start()
    query_loads[1].start()
    table_load.start()

    def rotated(raw, head_gain, cosine, sine):
        mean_square = jnp.mean(raw * raw, axis=-1, keepdims=True)
        y = raw * lax.rsqrt(mean_square + EPS) * head_gain
        return (y * cosine + pltpu.roll(y, HD // 2, 1) * sine).astype(jnp.bfloat16)

    base_c, base_s = far_c[pl.ds(ctx, 1), :], far_s[pl.ds(ctx, 1), :]
    cosine = near_c[...] * base_c - near_s[...] * base_s
    sine = near_s[...] * base_c + near_c[...] * base_s

    key_load.wait()
    value_load.wait()
    kv = jnp.dot(x[...], wkv[...], preferred_element_type=jnp.float32)
    kbuf[ctx] = rotated(kv[:, :HD], k_gain[...], cosine, sine)
    vbuf[ctx] = kv[:, HD:].T.astype(jnp.bfloat16)

    pl.semaphore_wait(barrier, NCTX + NTP - 2)

    def block(zz, yy, cc):
        return zz * 4 + yy * 2 + cc

    zp, zm, z2 = (z + 1) % 4, (z + 3) % 4, (z + 2) % 4
    sib = block(z, yh, 1 - core)
    up, down, across = block(zp, yh, core), block(zm, yh, core), block(z, 1 - yh, core)
    late_left, late_right, late_far = (block(n, 1 - yh, core) for n in (zm, zp, z2))
    sent = []

    def block_copy(kind, n, b, to):
        buffer, out_sem, in_sem = (kbuf, ks, kr) if kind == "k" else (vbuf, vs, vr)
        return remote(buffer.at[b], buffer.at[b], out_sem.at[n], in_sem.at[b], to, tp)

    def send(kind, b, to):
        n = sum(1 for item in sent if item[0] == kind)
        block_copy(kind, n, b, to).start()
        sent.append((kind, n, b, to))

    def arrived(kind, b):
        block_copy(kind, 0, b, sib).wait_recv()

    def hop_own():
        send("k", ctx, up)
        send("v", ctx, down)
        send("k", ctx, across)
        send("v", ctx, across)
        send("v", ctx, up)
        send("k", ctx, down)
        send("k", ctx, sib)
        send("v", ctx, sib)

    def hop_ring():
        left, right = block(zm, yh, core), block(zp, yh, core)
        arrived("k", left)
        send("k", left, up)
        arrived("v", right)
        send("v", right, down)
        arrived("v", left)
        arrived("k", right)
        for b in (left, right):
            send("k", b, sib)
            send("v", b, sib)

    def hop_across():
        arrived("k", across)
        arrived("v", across)
        for to in (up, down, sib):
            send("k", across, to)
            send("v", across, to)

    def hop_last(b, *more):
        arrived("k", b)
        arrived("v", b)
        for to in (*more, sib):
            send("k", b, to)
            send("v", b, to)

    def from_sib(zz, yy):
        arrived("k", block(zz, yy, 1 - core))
        arrived("v", block(zz, yy, 1 - core))

    hop_own()

    light = chip < 4
    moved = pick(chip, TAKEN)
    partner = block(3 - z, yh, core)
    kept = jnp.where(light, HEADS, HEADS - moved)

    def project_queries(first):
        raw = jnp.dot(x[...], wq[:, first * HD:(first + 4) * HD], preferred_element_type=jnp.float32)
        for h in range(4):
            q[first + h] = rotated(raw[:, h * HD:(h + 1) * HD], q_gain[...], cosine, sine)

    query_loads[0].wait()
    project_queries(4)

    def query_copy(f):
        return remote(q.at[kept + f], q.at[HEADS + f], qs.at[f], qr.at[f], partner, tp)

    hop_ring()
    query_loads[1].wait()
    project_queries(0)
    hop_across()

    @pl.when(jnp.logical_not(light))
    def _():
        @pl.loop(0, moved)
        def _(f):
            query_copy(f).start()

    table_load.wait()
    first_row = (ctx * NTP + tp) * VROWS
    lanes = (lax.broadcasted_iota(jnp.int32, (16, VROWS), 1) + first_row).astype(jnp.float32)
    down = lax.broadcasted_iota(jnp.int32, (16, 16), 0)
    sample = down % 8 * 2 + down // 8
    chosen = sample == lax.broadcasted_iota(jnp.int32, (16, 16), 1)
    picks = []
    for j in range(4):
        wanted = jnp.where(chosen, ids[j:j + 1, :].astype(jnp.float32), 0.0)
        picks.append((jnp.sum(wanted, axis=1, keepdims=True) == lanes).astype(jnp.float32))
    for c in range(2):
        rows = jnp.concatenate([p[c * 8:(c + 1) * 8] for p in picks], axis=0).astype(jnp.bfloat16)
        for n in range(NTP):
            cols = slice(n * PIECE, (n + 1) * PIECE)
            es[c, n] = jnp.dot(rows, tab[:, cols], preferred_element_type=jnp.float32).astype(jnp.bfloat16)

    def core_copy():
        return remote(es.at[1 - core], e0, e1s.at[0], e0r, sib, tp)

    core_copy().start()

    def pair_keys(j):
        return kbuf[pl.ds(2 * j, 2)].reshape(PAIR, HD)

    def with_ones(values):
        return jnp.concatenate([values, jnp.ones((16, values.shape[1]), jnp.bfloat16)], axis=0)

    def pair_values(j):
        return with_ones(jnp.concatenate([vbuf[2 * j], vbuf[2 * j + 1]], axis=1))

    def scores(keys, queries):
        return lax.dot_general(keys, queries, (((1,), (1,)), ((), ())), preferred_element_type=jnp.float32)

    def pipeline(units):
        held, mixed = {}, {}
        count = len(units)
        for t in range(count + 2):
            if t < count:
                held[t] = units[t][0]()
            if 0 <= t - 2:
                units[t - 2][2](mixed.pop(t - 2))
            if 0 <= t - 1 < count:
                mixed[t - 1] = units[t - 1][1](held.pop(t - 1))

    def causal(s):
        down = lax.broadcasted_iota(jnp.int32, s.shape, 0)
        return jnp.where(down <= lax.broadcasted_iota(jnp.int32, s.shape, 1), s, LOW)

    def open_unit(source, slot):
        def first():
            return scores(kbuf[ctx], q[source])

        def second(s):
            s = causal(s)
            peak = jnp.max(s, axis=0, keepdims=True) * SCALE
            top[slot, :1, :] = peak
            return jnp.exp2(s * SCALE - peak).astype(jnp.bfloat16)

        def third(w):
            acc[slot] = jnp.dot(with_ones(vbuf[ctx]), w, preferred_element_type=jnp.float32)

        return first, second, third

    def next_unit(keys, values, source, slot, mask=None):
        def first():
            return scores(keys(), q[source])

        def second(s):
            if mask is not None:
                s = mask(s)
            before = top[slot, :1, :]
            peak = jnp.maximum(before, jnp.max(s, axis=0, keepdims=True) * SCALE)
            top[slot, :1, :] = peak
            return jnp.exp2(s * SCALE - peak).astype(jnp.bfloat16), jnp.exp2(before - peak)

        def third(weights):
            w, factor = weights
            acc[slot] = acc[slot] * factor + jnp.dot(values(), w, preferred_element_type=jnp.float32)

        return first, second, third

    def pair_unit(j, source, slot):
        return next_unit(lambda: pair_keys(j), lambda: pair_values(j), source, slot)

    def block_unit(b, source, slot, mask=None):
        return next_unit(lambda: kbuf[b], lambda: with_ones(vbuf[b]), source, slot, mask)

    def open_heads(begin, width, count):
        places = []
        for n in range(width):
            use = n < count
            places.append((jnp.where(use, begin + n, 0), jnp.where(use, begin + n, SPARE)))

        @pl.when(core == 0)
        def _():
            pipeline([open_unit(*place) for place in places])

        @pl.when(core == 1)
        def _():
            pipeline([open_unit(*place) for place in places] + [block_unit(sib, *place) for place in places])

    arrived("k", sib)
    arrived("v", sib)
    hop_last(block(z2, yh, core), across)
    open_heads(chip * 0, 4, kept)
    core_copy().wait_recv()
    for n in range(NTP):
        e0[n] = (e0[n].astype(jnp.float32) + es[core, n].astype(jnp.float32)).astype(jnp.bfloat16)
    er[tp] = e0[tp]

    def token_copy(i, to, frm):
        return remote(e0.at[to], er.at[frm], e1s.at[i], e1r.at[frm], ctx, to)

    @pl.loop(1, NTP)
    def _(i):
        token_copy(i, (tp + i) % NTP, tp).start()

    @pl.when(kept > 6)
    def _():
        open_heads(chip * 0 + 4, 4, kept - 4)

    @pl.when(kept <= 6)
    def _():
        open_heads(chip * 0 + 4, 2, kept - 4)

    hop_last(late_left)
    hop_last(late_right)
    for zz, yy in ((z, 1 - yh), (zm, yh), (zp, yh), (z2, yh)):
        from_sib(zz, yy)

    @pl.when(light)
    def _():
        @pl.loop(0, moved)
        def _(f):
            acc[HEADS + f] = jnp.zeros((ACC, ROWS), jnp.float32)
            top[HEADS + f] = jnp.full((8, ROWS), LOW, jnp.float32)

    acc[SPARE] = jnp.zeros((ACC, ROWS), jnp.float32)
    top[SPARE] = jnp.zeros((8, ROWS), jnp.float32)

    counts = [pick(chip, [lists[n][0] for lists in PAIR_LISTS]) for n in range(4)]
    codes = [pick(chip, [lists[n][1] for lists in PAIR_LISTS]) for n in range(4)]
    widths = [kept, moved, moved, kept]
    soon_units = counts[0] * kept + counts[1] * moved
    all_units = soon_units + counts[2] * moved + counts[3] * kept
    late_group = soon_units // GROUP

    def choose(turn, values):
        result = values[0]
        for n in range(1, 4):
            result = jnp.where(turn == n, values[n], result)
        return result

    def settle(turn, k, h):
        for n in range(4):
            end = (turn == n) & (k >= counts[n])
            turn = jnp.where(end, n + 1, turn)
            k = jnp.where(end, 0, k)
        return turn, k, h

    def sample_copy(i, to, frm):
        return remote(eb.at[to], ec.at[frm], e2s.at[i], e2r.at[frm], to * 2 + core, tp)

    def sum_tokens():
        @pl.loop(1, NTP)
        def _(i):
            frm = (tp + i) % NTP
            token_copy(i, frm, frm).wait_recv()

        piece = er[0].astype(jnp.float32)
        for n in range(1, NTP):
            piece = piece + er[n].astype(jnp.float32)
        piece = jnp.dot(spread[...], piece.astype(jnp.bfloat16), preferred_element_type=jnp.float32)
        eb[...] = piece.astype(jnp.bfloat16).reshape(8, 16, PIECE)
        ec[chip] = eb[chip]

        @pl.loop(1, 8)
        def _(i):
            sample_copy(i, (chip + i) % 8, chip).start()

    def piece_copy(i, to, frm):
        return remote(eh.at[frm], eh.at[frm], e3s.at[i], e3r.at[frm], ctx, to)

    def sum_samples():
        @pl.loop(1, 8)
        def _(i):
            frm = (chip + i) % 8
            sample_copy(i, frm, frm).wait_recv()

        piece = ec[0].astype(jnp.float32)
        for n in range(1, 8):
            piece = piece + ec[n].astype(jnp.float32)
        eh[tp] = piece.astype(jnp.bfloat16)

        @pl.loop(1, NTP)
        def _(i):
            piece_copy(i, (tp + i) % NTP, tp).start()

    def between(g):
        @pl.when(light & (g == jnp.minimum(chip, 1)))
        def _():
            @pl.loop(0, moved)
            def _(f):
                query_copy(f).wait_recv()

        @pl.when(g == 1)
        def _():
            hop_last(late_far)
            sum_tokens()

        @pl.when(g == late_group)
        def _():
            for zz in (zm, zp, z2):
                from_sib(zz, 1 - yh)

        @pl.when(g == late_group + 1)
        def _():
            sum_samples()

    def step(g, state):
        between(g)
        units = []
        for n in range(GROUP):
            turn, k, h = state
            use = turn < 4
            j = lax.shift_right_logical(choose(turn, codes), 3 * k) % 8
            slot = h + jnp.where((turn == 1) | (turn == 2), HEADS, 0 * h)
            units.append(pair_unit(jnp.where(use, j, chip), jnp.where(use, slot, 0), jnp.where(use, slot, SPARE)))
            h = h + 1
            wrap = h >= choose(turn, widths)
            state = settle(turn, k + wrap.astype(jnp.int32), jnp.where(wrap, 0, h))
        pipeline(units)
        return state

    lax.fori_loop(0, (all_units + GROUP - 1) // GROUP, step, settle(chip * 0, chip * 0, chip * 0))

    def finished(slot):
        mix = acc[slot]
        return (mix[:HD] * (1.0 / mix[HD:HD + 1])).T.astype(jnp.bfloat16)

    def result_copy(f):
        return remote(fsend.at[f], frecv.at[f], fs.at[f], fr.at[f], partner, tp)

    @pl.when(light)
    def _():
        def close_heads(width):
            places = []
            for f in range(width):
                use = f < moved
                slot = HEADS + f + 0 * chip
                places.append((jnp.where(use, slot, 0), jnp.where(use, slot, SPARE)))

            @pl.when(core == 0)
            def _():
                pipeline([block_unit(partner, *place, causal) for place in places])

            @pl.when(core == 1)
            def _():
                pipeline(
                    [block_unit(partner, *place, causal) for place in places]
                    + [block_unit(partner - 1, *place) for place in places]
                )

        @pl.when(moved == 1)
        def _():
            close_heads(1)

        @pl.when(moved > 1)
        def _():
            close_heads(3)

        @pl.loop(0, moved)
        def _(f):
            fsend[f] = finished(HEADS + f)
            result_copy(f).start()

    @pl.loop(1, NTP)
    def _(i):
        frm = (tp + i) % NTP
        piece_copy(i, frm, frm).wait_recv()

    hidden = jnp.concatenate([eh[n] for n in range(NTP)], axis=1).astype(jnp.float32)
    xs[...] = normed(hidden)
    step_c, step_s = far_c[NCTX:NCTX + 1, :], far_s[NCTX:NCTX + 1, :]
    dec_c = near_c[:16, :] * step_c - near_s[:16, :] * step_s
    dec_s = near_s[:16, :] * step_c + near_c[:16, :] * step_s
    step_kv = jnp.dot(xs[...], wkv[...], preferred_element_type=jnp.float32)
    step_k = rotated(step_kv[:, :HD], k_gain[...], dec_c, dec_s)
    step_v = step_kv[:, HD:].astype(jnp.bfloat16)
    for g in range(2):
        raw = jnp.dot(xs[...], wq[:, g * 512:(g + 1) * 512], preferred_element_type=jnp.float32)
        for h in range(4):
            rows = slice((g * 4 + h) * 16, (g * 4 + h + 1) * 16)
            qd[rows, :] = rotated(raw[:, h * HD:(h + 1) * HD], q_gain[...], dec_c, dec_s)

    own = scores(step_k, qd[...])
    step = lax.broadcasted_iota(jnp.int32, (16, HD), 1) % 16
    own = jnp.where(lax.broadcasted_iota(jnp.int32, (16, HD), 0) <= step, own, LOW)
    peak = jnp.max(own, axis=0, keepdims=True) * SCALE
    weights = jnp.exp2(own * SCALE - peak).astype(jnp.bfloat16)
    topd[:1, :] = peak
    step_values = jnp.concatenate([step_v, jnp.ones((16, 16), jnp.bfloat16)], axis=1)
    accd[...] = lax.dot_general(
        step_values, weights, (((0,), (0,)), ((), ())), preferred_element_type=jnp.float32
    )

    def step_unit(j):
        def first():
            return scores(pair_keys(j), qd[...])

        def second(s):
            before = topd[:1, :]
            peak = jnp.maximum(before, jnp.max(s, axis=0, keepdims=True) * SCALE)
            topd[:1, :] = peak
            return jnp.exp2(s * SCALE - peak).astype(jnp.bfloat16), jnp.exp2(before - peak)

        def third(weights):
            w, factor = weights
            accd[...] = accd[...] * factor + jnp.dot(pair_values(j), w, preferred_element_type=jnp.float32)

        return first, second, third

    pipeline([step_unit(j) for j in range(8)])
    mix = accd[...]
    steps = (mix[:HD] * (1.0 / mix[HD:HD + 1])).T.astype(jnp.bfloat16)
    for h in range(HEADS):
        dec[:, h * HD:(h + 1) * HD] = steps[h * 16:(h + 1) * 16, :]

    @pl.loop(0, kept)
    def _(h):
        out[:, pl.ds(pl.multiple_of(h * HD, HD), HD)] = finished(h)

    @pl.when(jnp.logical_not(light))
    def _():
        @pl.loop(0, moved)
        def _(f):
            result_copy(f).wait_recv()
            out[:, pl.ds(pl.multiple_of((kept + f) * HD, HD), HD)] = frecv[f]
            query_copy(f).wait_send()

    @pl.when(light)
    def _():
        @pl.loop(0, moved)
        def _(f):
            result_copy(f).wait_send()

    for item in sent:
        block_copy(*item).wait_send()

    core_copy().wait_send()

    @pl.loop(1, NTP)
    def _(i):
        to = (tp + i) % NTP
        token_copy(i, to, tp).wait_send()
        piece_copy(i, to, tp).wait_send()

    @pl.loop(1, 8)
    def _(i):
        sample_copy(i, (chip + i) % 8, chip).wait_send()


def body(prompt, norm_gain, w_query, w_key, w_value, query_gain, key_gain, table, sampled):
    near_c, near_s, far_c, far_s = rope_tables(NCTX * ROWS)
    spread = np.zeros((8 * 16, 32), np.float32)
    for s in range(8):
        for j in range(4):
            spread[s * 16 + j, j * 8 + s] = 1.0
    hbm = pl.BlockSpec(memory_space=pl.ANY)
    vmem = pl.BlockSpec(memory_space=pltpu.VMEM)
    bf, f32 = jnp.bfloat16, jnp.float32
    dma = pltpu.SemaphoreType.DMA
    out, dec = pl.pallas_call(
        kernel,
        out_shape=(
            jax.ShapeDtypeStruct((ROWS, HEADS * HD), bf),
            jax.ShapeDtypeStruct((16, HEADS * HD), bf),
        ),
        in_specs=[hbm, vmem, hbm, hbm, hbm, vmem, vmem, hbm] + [vmem] * 6,
        out_specs=(vmem, vmem),
        scratch_shapes=[
            pltpu.VMEM((ROWS, D), bf),
            pltpu.VMEM((D, HEADS * HD), bf),
            pltpu.VMEM((D, 2 * HD), bf),
            pltpu.VMEM((VROWS, D), bf),
            pltpu.VMEM((12, ROWS, HD), bf),
            pltpu.VMEM((NCTX, ROWS, HD), bf),
            pltpu.VMEM((NCTX, HD, ROWS), bf),
            pltpu.VMEM((SPARE + 1, ACC, ROWS), f32),
            pltpu.VMEM((SPARE + 1, 8, ROWS), f32),
            pltpu.VMEM((2, NTP, 32, PIECE), bf),
            pltpu.VMEM((NTP, 32, PIECE), bf),
            pltpu.VMEM((NTP, 32, PIECE), bf),
            pltpu.VMEM((8, 16, PIECE), bf),
            pltpu.VMEM((8, 16, PIECE), bf),
            pltpu.VMEM((NTP, 16, PIECE), bf),
            pltpu.VMEM((16, D), bf),
            pltpu.VMEM((HD, HD), bf),
            pltpu.VMEM((ACC, HD), f32),
            pltpu.VMEM((8, HD), f32),
            pltpu.VMEM((4, ROWS, HD), bf),
            pltpu.VMEM((4, ROWS, HD), bf),
            dma((7,)), dma((2,)),
            dma((16,)), dma((NCTX,)), dma((16,)), dma((NCTX,)),
            dma, dma((NTP,)), dma((NTP,)), dma((8,)), dma((8,)), dma((NTP,)), dma((NTP,)),
            dma((4,)), dma((4,)), dma((4,)), dma((4,)),
        ],
        compiler_params=pltpu.CompilerParams(
            collective_id=0, has_side_effects=True, vmem_limit_bytes=62 * 2**20
        ),
    )(
        prompt, norm_gain[None, :], w_query, w_key, w_value, query_gain[None, :], key_gain[None, :], table,
        sampled.T, near_c, near_s, far_c, far_s, spread.astype(jnp.bfloat16),
    )
    return out, dec[None, :4]


def solution(mesh):
    in_specs = (
        P("ctx", None),
        P(),
        P(None, "tp"),
        P(None, "tp"),
        P(None, "tp"),
        P(),
        P(),
        P(("ctx", "tp"), None),
        P(),
    )
    out_specs = (P("ctx", "tp"), P("ctx", None, "tp"))
    return jax.shard_map(body, mesh=mesh, in_specs=in_specs, out_specs=out_specs, check_vma=False)
```

```python
import functools

import jax
import jax.numpy as jnp
import numpy as np
from jax import lax
from jax.experimental import pallas as pl
from jax.experimental.pallas import tpu as pltpu
from jax.sharding import PartitionSpec as P

MESH = pl.DeviceIdType.MESH
EPS = 1e-06
THETA = 1000000.0
HD = 128
ROWS = 512
D = 5120
PAIR = 2 * ROWS
HEADS = 8
NCTX = 16
NTP = 8
VROWS = 608
PIECE = D // NTP
SCALE = HD ** (-0.5) * 1.4426950408889634
LOW = -1e30
GROUP = 5
SPARE = 11
TAKEN = (3, 3, 2, 1, 2, 1, 3, 3)
ACC = HD + 16


def rope_tables(prompt_len):
    half = HD // 2
    freqs = THETA ** (-np.arange(half, dtype=np.float64) / half)
    freqs = np.concatenate([freqs, freqs])[None, :]
    sign = np.concatenate([-np.ones(half), np.ones(half)])[None, :]
    near = np.arange(ROWS, dtype=np.float64)[:, None] * freqs
    far = (np.arange(prompt_len // ROWS + 1, dtype=np.float64) * ROWS)[:, None] * freqs
    tables = (np.cos(near), np.sin(near) * sign, np.cos(far), np.sin(far) * sign)
    return [t.astype(np.float32) for t in tables]


def pair_lists(chip):
    zz, yy = chip // 2, chip % 2
    at = lambda dz, y: (zz + dz) % 4 * 2 + y
    soon = [at(0, 1 - yy), at(3, yy), at(1, yy), at(2, yy)]
    late = [at(3, 1 - yy), at(1, 1 - yy), at(2, 1 - yy)]
    cut = lambda pairs, limit: [j for j in pairs if j < limit]
    other = (3 - zz) * 2 + yy if chip < 4 else -1
    lists = [cut(soon, chip), cut([chip] + soon, other), cut(late, other), cut(late, chip)]
    return [(len(pairs), sum(j << (3 * k) for k, j in enumerate(pairs))) for pairs in lists]


PAIR_LISTS = [pair_lists(chip) for chip in range(8)]


def pick(index, values):
    result = index * 0 + values[-1]
    for n, value in enumerate(values[:-1]):
        result = result + (index == n).astype(jnp.int32) * (value - values[-1])
    return result


def kernel(
    prompt, gain, w_query, w_key, w_value, q_gain, k_gain, table, ids, near_c, near_s, far_c, far_s, spread,
    out, dec,
    x, wq, wkv, tab, q, kbuf, vbuf, acc, top, es, e0, er, eb, ec, eh, xs, qd, accd, topd, fsend, frecv,
    load_sem, wq_sem, ks, kr, vs, vr, e0r, e1s, e1r, e2s, e2r, e3s, e3r, qs, qr, fs, fr,
):
    ctx = lax.axis_index("ctx")
    tp = lax.axis_index("tp")
    chip = ctx // 2
    core = ctx % 2
    z = ctx // 4
    yh = chip % 2

    def remote(src, dst, send, recv, to_ctx, to_tp):
        return pltpu.make_async_remote_copy(
            src_ref=src, dst_ref=dst, send_sem=send, recv_sem=recv,
            device_id=(to_ctx, to_tp), device_id_type=MESH,
        )

    prompt_loads = []
    for n in range(4):
        rows = pl.ds(n * 128, 128)
        prompt_loads.append(pltpu.make_async_copy(prompt.at[rows], x.at[rows], load_sem.at[n]))
    key_load = pltpu.make_async_copy(w_key, wkv.at[:, pl.ds(0, HD)], load_sem.at[4])
    value_load = pltpu.make_async_copy(w_value, wkv.at[:, pl.ds(HD, HD)], load_sem.at[5])
    table_load = pltpu.make_async_copy(table, tab, load_sem.at[6])
    query_loads = []
    for n in range(2):
        cols = pl.ds((1 - n) * 512, 512)
        query_loads.append(pltpu.make_async_copy(w_query.at[:, cols], wq.at[:, cols], wq_sem.at[n]))
    for load in (*prompt_loads, key_load, value_load):
        load.start()

    barrier = pltpu.get_barrier_semaphore()

    @pl.loop(1, NCTX)
    def _(i):
        pl.semaphore_signal(barrier, inc=1, device_id=((ctx + i) % NCTX, tp), device_id_type=MESH)

    @pl.loop(1, NTP)
    def _(i):
        pl.semaphore_signal(barrier, inc=1, device_id=(ctx, (tp + i) % NTP), device_id_type=MESH)

    def normed(rows_f32):
        mean_square = jnp.mean(rows_f32 * rows_f32, axis=-1, keepdims=True)
        return (rows_f32 * lax.rsqrt(mean_square + EPS) * gain[...]).astype(jnp.bfloat16)

    for n in range(4):
        prompt_loads[n].wait()

        @pl.loop(0, 8, unroll=2)
        def _(i):
            rows = pl.ds(pl.multiple_of(n * 128 + i * 16, 16), 16)
            x[rows, :] = normed(x[rows, :].astype(jnp.float32))

        if n == 2:
            query_loads[0].start()
    query_loads[1].start()
    table_load.start()

    def rotated(raw, head_gain, cosine, sine):
        mean_square = jnp.mean(raw * raw, axis=-1, keepdims=True)
        y = raw * lax.rsqrt(mean_square + EPS) * head_gain
        return (y * cosine + pltpu.roll(y, HD // 2, 1) * sine).astype(jnp.bfloat16)

    base_c, base_s = far_c[pl.ds(ctx, 1), :], far_s[pl.ds(ctx, 1), :]
    cosine = near_c[...] * base_c - near_s[...] * base_s
    sine = near_s[...] * base_c + near_c[...] * base_s

    key_load.wait()
    value_load.wait()
    kv = jnp.dot(x[...], wkv[...], preferred_element_type=jnp.float32)
    kbuf[ctx] = rotated(kv[:, :HD], k_gain[...], cosine, sine)
    vbuf[ctx] = kv[:, HD:].T.astype(jnp.bfloat16)

    pl.semaphore_wait(barrier, NCTX + NTP - 2)

    def block(zz, yy, cc):
        return zz * 4 + yy * 2 + cc

    zp, zm, z2 = (z + 1) % 4, (z + 3) % 4, (z + 2) % 4
    sib = block(z, yh, 1 - core)
    up, down, across = block(zp, yh, core), block(zm, yh, core), block(z, 1 - yh, core)
    late_left, late_right, late_far = (block(n, 1 - yh, core) for n in (zm, zp, z2))
    sent = []

    def block_copy(kind, n, b, to):
        buffer, out_sem, in_sem = (kbuf, ks, kr) if kind == "k" else (vbuf, vs, vr)
        return remote(buffer.at[b], buffer.at[b], out_sem.at[n], in_sem.at[b], to, tp)

    def send(kind, b, to):
        n = sum(1 for item in sent if item[0] == kind)
        block_copy(kind, n, b, to).start()
        sent.append((kind, n, b, to))

    def arrived(kind, b):
        block_copy(kind, 0, b, sib).wait_recv()

    def hop_own():
        send("k", ctx, up)
        send("v", ctx, down)
        send("k", ctx, across)
        send("v", ctx, across)
        send("v", ctx, up)
        send("k", ctx, down)
        send("k", ctx, sib)
        send("v", ctx, sib)

    def hop_ring():
        left, right = block(zm, yh, core), block(zp, yh, core)
        arrived("k", left)
        send("k", left, up)
        arrived("v", right)
        send("v", right, down)
        arrived("v", left)
        arrived("k", right)
        for b in (left, right):
            send("k", b, sib)
            send("v", b, sib)

    def hop_across():
        arrived("k", across)
        arrived("v", across)
        for to in (up, down, sib):
            send("k", across, to)
            send("v", across, to)

    def hop_last(b, *more):
        arrived("k", b)
        arrived("v", b)
        for to in (*more, sib):
            send("k", b, to)
            send("v", b, to)

    def from_sib(zz, yy):
        arrived("k", block(zz, yy, 1 - core))
        arrived("v", block(zz, yy, 1 - core))

    hop_own()

    light = chip < 4
    moved = pick(chip, TAKEN)
    partner = block(3 - z, yh, core)
    kept = jnp.where(light, HEADS, HEADS - moved)

    def project_queries(first):
        raw = jnp.dot(x[...], wq[:, first * HD:(first + 4) * HD], preferred_element_type=jnp.float32)
        for h in range(4):
            q[first + h] = rotated(raw[:, h * HD:(h + 1) * HD], q_gain[...], cosine, sine)

    query_loads[0].wait()
    project_queries(4)

    def query_copy(f):
        return remote(q.at[kept + f], q.at[HEADS + f], qs.at[f], qr.at[f], partner, tp)

    hop_ring()
    query_loads[1].wait()
    project_queries(0)
    hop_across()

    @pl.when(jnp.logical_not(light))
    def _():
        @pl.loop(0, moved)
        def _(f):
            query_copy(f).start()


    def pair_keys(j):
        return kbuf[pl.ds(2 * j, 2)].reshape(PAIR, HD)

    def with_ones(values):
        return jnp.concatenate([values, jnp.ones((16, values.shape[1]), jnp.bfloat16)], axis=0)

    def pair_values(j):
        return with_ones(jnp.concatenate([vbuf[2 * j], vbuf[2 * j + 1]], axis=1))

    def scores(keys, queries):
        return lax.dot_general(keys, queries, (((1,), (1,)), ((), ())), preferred_element_type=jnp.float32)

    def pipeline(units):
        held, mixed = {}, {}
        count = len(units)
        for t in range(count + 2):
            if t < count:
                held[t] = units[t][0]()
            if 0 <= t - 2:
                units[t - 2][2](mixed.pop(t - 2))
            if 0 <= t - 1 < count:
                mixed[t - 1] = units[t - 1][1](held.pop(t - 1))

    def causal(s):
        down = lax.broadcasted_iota(jnp.int32, s.shape, 0)
        return jnp.where(down <= lax.broadcasted_iota(jnp.int32, s.shape, 1), s, LOW)

    def open_unit(source, slot):
        def first():
            return scores(kbuf[ctx], q[source])

        def second(s):
            s = causal(s)
            peak = jnp.max(s, axis=0, keepdims=True) * SCALE
            top[slot, :1, :] = peak
            return jnp.exp2(s * SCALE - peak).astype(jnp.bfloat16)

        def third(w):
            acc[slot] = jnp.dot(with_ones(vbuf[ctx]), w, preferred_element_type=jnp.float32)

        return first, second, third

    def next_unit(keys, values, source, slot, mask=None):
        def first():
            return scores(keys(), q[source])

        def second(s):
            if mask is not None:
                s = mask(s)
            before = top[slot, :1, :]
            peak = jnp.maximum(before, jnp.max(s, axis=0, keepdims=True) * SCALE)
            top[slot, :1, :] = peak
            return jnp.exp2(s * SCALE - peak).astype(jnp.bfloat16), jnp.exp2(before - peak)

        def third(weights):
            w, factor = weights
            acc[slot] = acc[slot] * factor + jnp.dot(values(), w, preferred_element_type=jnp.float32)

        return first, second, third

    def pair_unit(j, source, slot):
        return next_unit(lambda: pair_keys(j), lambda: pair_values(j), source, slot)

    def block_unit(b, source, slot, mask=None):
        return next_unit(lambda: kbuf[b], lambda: with_ones(vbuf[b]), source, slot, mask)

    def open_heads(begin, width, count):
        places = []
        for n in range(width):
            use = n < count
            places.append((jnp.where(use, begin + n, 0), jnp.where(use, begin + n, SPARE)))

        @pl.when(core == 0)
        def _():
            pipeline([open_unit(*place) for place in places])

        @pl.when(core == 1)
        def _():
            pipeline([open_unit(*place) for place in places] + [block_unit(sib, *place) for place in places])

    arrived("k", sib)
    arrived("v", sib)
    hop_last(block(z2, yh, core), across)
    open_heads(chip * 0, 4, kept)

    table_load.wait()
    first_row = (ctx * NTP + tp) * VROWS
    lanes = (lax.broadcasted_iota(jnp.int32, (16, VROWS), 1) + first_row).astype(jnp.float32)
    down = lax.broadcasted_iota(jnp.int32, (16, 16), 0)
    sample = down % 8 * 2 + down // 8
    chosen = sample == lax.broadcasted_iota(jnp.int32, (16, 16), 1)
    picks = []
    for j in range(4):
        wanted = jnp.where(chosen, ids[j:j + 1, :].astype(jnp.float32), 0.0)
        picks.append((jnp.sum(wanted, axis=1, keepdims=True) == lanes).astype(jnp.float32))
    for c in range(2):
        rows = jnp.concatenate([p[c * 8:(c + 1) * 8] for p in picks], axis=0).astype(jnp.bfloat16)
        for n in range(NTP):
            cols = slice(n * PIECE, (n + 1) * PIECE)
            es[c, n] = jnp.dot(rows, tab[:, cols], preferred_element_type=jnp.float32).astype(jnp.bfloat16)

    def core_copy():
        return remote(es.at[1 - core], e0, e1s.at[0], e0r, sib, tp)

    core_copy().start()

    @pl.when(kept > 6)
    def _():
        open_heads(chip * 0 + 4, 4, kept - 4)

    @pl.when(kept <= 6)
    def _():
        open_heads(chip * 0 + 4, 2, kept - 4)

    core_copy().wait_recv()
    for n in range(NTP):
        e0[n] = (e0[n].astype(jnp.float32) + es[core, n].astype(jnp.float32)).astype(jnp.bfloat16)
    er[tp] = e0[tp]

    def token_copy(i, to, frm):
        return remote(e0.at[to], er.at[frm], e1s.at[i], e1r.at[frm], ctx, to)

    @pl.loop(1, NTP)
    def _(i):
        token_copy(i, (tp + i) % NTP, tp).start()

    for zz, yy in ((z, 1 - yh), (zm, yh), (zp, yh), (z2, yh)):
        from_sib(zz, yy)

    @pl.when(light)
    def _():
        @pl.loop(0, moved)
        def _(f):
            acc[HEADS + f] = jnp.zeros((ACC, ROWS), jnp.float32)
            top[HEADS + f] = jnp.full((8, ROWS), LOW, jnp.float32)

    acc[SPARE] = jnp.zeros((ACC, ROWS), jnp.float32)
    top[SPARE] = jnp.zeros((8, ROWS), jnp.float32)

    counts = [pick(chip, [lists[n][0] for lists in PAIR_LISTS]) for n in range(4)]
    codes = [pick(chip, [lists[n][1] for lists in PAIR_LISTS]) for n in range(4)]
    widths = [kept, moved, moved, kept]
    soon_units = counts[0] * kept + counts[1] * moved
    all_units = soon_units + counts[2] * moved + counts[3] * kept
    late_group = soon_units // GROUP

    def choose(turn, values):
        result = values[0]
        for n in range(1, 4):
            result = jnp.where(turn == n, values[n], result)
        return result

    def settle(turn, k, h):
        for n in range(4):
            end = (turn == n) & (k >= counts[n])
            turn = jnp.where(end, n + 1, turn)
            k = jnp.where(end, 0, k)
        return turn, k, h

    def sample_copy(i, to, frm):
        return remote(eb.at[to], ec.at[frm], e2s.at[i], e2r.at[frm], to * 2 + core, tp)

    def sum_tokens():
        @pl.loop(1, NTP)
        def _(i):
            frm = (tp + i) % NTP
            token_copy(i, frm, frm).wait_recv()

        piece = er[0].astype(jnp.float32)
        for n in range(1, NTP):
            piece = piece + er[n].astype(jnp.float32)
        piece = jnp.dot(spread[...], piece.astype(jnp.bfloat16), preferred_element_type=jnp.float32)
        eb[...] = piece.astype(jnp.bfloat16).reshape(8, 16, PIECE)
        ec[chip] = eb[chip]

        @pl.loop(1, 8)
        def _(i):
            sample_copy(i, (chip + i) % 8, chip).start()

    def piece_copy(i, to, frm):
        return remote(eh.at[frm], eh.at[frm], e3s.at[i], e3r.at[frm], ctx, to)

    def sum_samples():
        @pl.loop(1, 8)
        def _(i):
            frm = (chip + i) % 8
            sample_copy(i, frm, frm).wait_recv()

        piece = ec[0].astype(jnp.float32)
        for n in range(1, 8):
            piece = piece + ec[n].astype(jnp.float32)
        eh[tp] = piece.astype(jnp.bfloat16)

        @pl.loop(1, NTP)
        def _(i):
            piece_copy(i, (tp + i) % NTP, tp).start()

    def between(g):
        @pl.when(light & (g == jnp.minimum(chip, 1)))
        def _():
            @pl.loop(0, moved)
            def _(f):
                query_copy(f).wait_recv()

        @pl.when(g == 1)
        def _():
            hop_last(late_left)
            hop_last(late_right)
            hop_last(late_far)

        @pl.when(g == 2)
        def _():
            sum_tokens()

        @pl.when(g == late_group)
        def _():
            for zz in (zm, zp, z2):
                from_sib(zz, 1 - yh)

        @pl.when(g == late_group + 1)
        def _():
            sum_samples()

    def step(g, state):
        between(g)
        units = []
        for n in range(GROUP):
            turn, k, h = state
            use = turn < 4
            j = lax.shift_right_logical(choose(turn, codes), 3 * k) % 8
            slot = h + jnp.where((turn == 1) | (turn == 2), HEADS, 0 * h)
            units.append(pair_unit(jnp.where(use, j, chip), jnp.where(use, slot, 0), jnp.where(use, slot, SPARE)))
            h = h + 1
            wrap = h >= choose(turn, widths)
            state = settle(turn, k + wrap.astype(jnp.int32), jnp.where(wrap, 0, h))
        pipeline(units)
        return state

    lax.fori_loop(0, (all_units + GROUP - 1) // GROUP, step, settle(chip * 0, chip * 0, chip * 0))

    def finished(slot):
        mix = acc[slot]
        return (mix[:HD] * (1.0 / mix[HD:HD + 1])).T.astype(jnp.bfloat16)

    def result_copy(f):
        return remote(fsend.at[f], frecv.at[f], fs.at[f], fr.at[f], partner, tp)

    @pl.when(light)
    def _():
        def close_heads(width):
            places = []
            for f in range(width):
                use = f < moved
                slot = HEADS + f + 0 * chip
                places.append((jnp.where(use, slot, 0), jnp.where(use, slot, SPARE)))

            @pl.when(core == 0)
            def _():
                pipeline([block_unit(partner, *place, causal) for place in places])

            @pl.when(core == 1)
            def _():
                pipeline(
                    [block_unit(partner, *place, causal) for place in places]
                    + [block_unit(partner - 1, *place) for place in places]
                )

        @pl.when(moved == 1)
        def _():
            close_heads(1)

        @pl.when(moved > 1)
        def _():
            close_heads(3)

        @pl.loop(0, moved)
        def _(f):
            fsend[f] = finished(HEADS + f)
            result_copy(f).start()

    @pl.loop(1, NTP)
    def _(i):
        frm = (tp + i) % NTP
        piece_copy(i, frm, frm).wait_recv()

    hidden = jnp.concatenate([eh[n] for n in range(NTP)], axis=1).astype(jnp.float32)
    xs[...] = normed(hidden)
    step_c, step_s = far_c[NCTX:NCTX + 1, :], far_s[NCTX:NCTX + 1, :]
    dec_c = near_c[:16, :] * step_c - near_s[:16, :] * step_s
    dec_s = near_s[:16, :] * step_c + near_c[:16, :] * step_s
    step_kv = jnp.dot(xs[...], wkv[...], preferred_element_type=jnp.float32)
    step_k = rotated(step_kv[:, :HD], k_gain[...], dec_c, dec_s)
    step_v = step_kv[:, HD:].astype(jnp.bfloat16)
    for g in range(2):
        raw = jnp.dot(xs[...], wq[:, g * 512:(g + 1) * 512], preferred_element_type=jnp.float32)
        for h in range(4):
            rows = slice((g * 4 + h) * 16, (g * 4 + h + 1) * 16)
            qd[rows, :] = rotated(raw[:, h * HD:(h + 1) * HD], q_gain[...], dec_c, dec_s)

    own = scores(step_k, qd[...])
    step = lax.broadcasted_iota(jnp.int32, (16, HD), 1) % 16
    own = jnp.where(lax.broadcasted_iota(jnp.int32, (16, HD), 0) <= step, own, LOW)
    peak = jnp.max(own, axis=0, keepdims=True) * SCALE
    weights = jnp.exp2(own * SCALE - peak).astype(jnp.bfloat16)
    topd[:1, :] = peak
    step_values = jnp.concatenate([step_v, jnp.ones((16, 16), jnp.bfloat16)], axis=1)
    accd[...] = lax.dot_general(
        step_values, weights, (((0,), (0,)), ((), ())), preferred_element_type=jnp.float32
    )

    def step_unit(j):
        def first():
            return scores(pair_keys(j), qd[...])

        def second(s):
            before = topd[:1, :]
            peak = jnp.maximum(before, jnp.max(s, axis=0, keepdims=True) * SCALE)
            topd[:1, :] = peak
            return jnp.exp2(s * SCALE - peak).astype(jnp.bfloat16), jnp.exp2(before - peak)

        def third(weights):
            w, factor = weights
            accd[...] = accd[...] * factor + jnp.dot(pair_values(j), w, preferred_element_type=jnp.float32)

        return first, second, third

    pipeline([step_unit(j) for j in range(8)])
    mix = accd[...]
    steps = (mix[:HD] * (1.0 / mix[HD:HD + 1])).T.astype(jnp.bfloat16)
    for h in range(HEADS):
        dec[:, h * HD:(h + 1) * HD] = steps[h * 16:(h + 1) * 16, :]

    @pl.loop(0, kept)
    def _(h):
        out[:, pl.ds(pl.multiple_of(h * HD, HD), HD)] = finished(h)

    @pl.when(jnp.logical_not(light))
    def _():
        @pl.loop(0, moved)
        def _(f):
            result_copy(f).wait_recv()
            out[:, pl.ds(pl.multiple_of((kept + f) * HD, HD), HD)] = frecv[f]
            query_copy(f).wait_send()

    @pl.when(light)
    def _():
        @pl.loop(0, moved)
        def _(f):
            result_copy(f).wait_send()

    for item in sent:
        block_copy(*item).wait_send()

    core_copy().wait_send()

    @pl.loop(1, NTP)
    def _(i):
        to = (tp + i) % NTP
        token_copy(i, to, tp).wait_send()
        piece_copy(i, to, tp).wait_send()

    @pl.loop(1, 8)
    def _(i):
        sample_copy(i, (chip + i) % 8, chip).wait_send()


def body(prompt, norm_gain, w_query, w_key, w_value, query_gain, key_gain, table, sampled):
    near_c, near_s, far_c, far_s = rope_tables(NCTX * ROWS)
    spread = np.zeros((8 * 16, 32), np.float32)
    for s in range(8):
        for j in range(4):
            spread[s * 16 + j, j * 8 + s] = 1.0
    hbm = pl.BlockSpec(memory_space=pl.ANY)
    vmem = pl.BlockSpec(memory_space=pltpu.VMEM)
    bf, f32 = jnp.bfloat16, jnp.float32
    dma = pltpu.SemaphoreType.DMA
    out, dec = pl.pallas_call(
        kernel,
        out_shape=(
            jax.ShapeDtypeStruct((ROWS, HEADS * HD), bf),
            jax.ShapeDtypeStruct((16, HEADS * HD), bf),
        ),
        in_specs=[hbm, vmem, hbm, hbm, hbm, vmem, vmem, hbm] + [vmem] * 6,
        out_specs=(vmem, vmem),
        scratch_shapes=[
            pltpu.VMEM((ROWS, D), bf),
            pltpu.VMEM((D, HEADS * HD), bf),
            pltpu.VMEM((D, 2 * HD), bf),
            pltpu.VMEM((VROWS, D), bf),
            pltpu.VMEM((12, ROWS, HD), bf),
            pltpu.VMEM((NCTX, ROWS, HD), bf),
            pltpu.VMEM((NCTX, HD, ROWS), bf),
            pltpu.VMEM((SPARE + 1, ACC, ROWS), f32),
            pltpu.VMEM((SPARE + 1, 8, ROWS), f32),
            pltpu.VMEM((2, NTP, 32, PIECE), bf),
            pltpu.VMEM((NTP, 32, PIECE), bf),
            pltpu.VMEM((NTP, 32, PIECE), bf),
            pltpu.VMEM((8, 16, PIECE), bf),
            pltpu.VMEM((8, 16, PIECE), bf),
            pltpu.VMEM((NTP, 16, PIECE), bf),
            pltpu.VMEM((16, D), bf),
            pltpu.VMEM((HD, HD), bf),
            pltpu.VMEM((ACC, HD), f32),
            pltpu.VMEM((8, HD), f32),
            pltpu.VMEM((4, ROWS, HD), bf),
            pltpu.VMEM((4, ROWS, HD), bf),
            dma((7,)), dma((2,)),
            dma((16,)), dma((NCTX,)), dma((16,)), dma((NCTX,)),
            dma, dma((NTP,)), dma((NTP,)), dma((8,)), dma((8,)), dma((NTP,)), dma((NTP,)),
            dma((4,)), dma((4,)), dma((4,)), dma((4,)),
        ],
        compiler_params=pltpu.CompilerParams(
            collective_id=0, has_side_effects=True, vmem_limit_bytes=62 * 2**20
        ),
    )(
        prompt, norm_gain[None, :], w_query, w_key, w_value, query_gain[None, :], key_gain[None, :], table,
        sampled.T, near_c, near_s, far_c, far_s, spread.astype(jnp.bfloat16),
    )
    return out, dec[None, :4]


def solution(mesh):
    in_specs = (
        P("ctx", None),
        P(),
        P(None, "tp"),
        P(None, "tp"),
        P(None, "tp"),
        P(),
        P(),
        P(("ctx", "tp"), None),
        P(),
    )
    out_specs = (P("ctx", "tp"), P("ctx", None, "tp"))
    return jax.shard_map(body, mesh=mesh, in_specs=in_specs, out_specs=out_specs, check_vma=False)
```

```python
import functools

import jax
import jax.numpy as jnp
import numpy as np
from jax import lax
from jax.experimental import pallas as pl
from jax.experimental.pallas import tpu as pltpu
from jax.sharding import PartitionSpec as P

MESH = pl.DeviceIdType.MESH
EPS = 1e-06
THETA = 1000000.0
HD = 128
ROWS = 512
D = 5120
PAIR = 2 * ROWS
HEADS = 8
NCTX = 16
NTP = 8
VROWS = 608
PIECE = D // NTP
SCALE = HD ** (-0.5) * 1.4426950408889634
LOW = -1e30
GROUP = 5
SPARE = 11
TAKEN = (3, 3, 2, 1, 2, 1, 3, 3)
ACC = HD + 16


def rope_tables(prompt_len):
    half = HD // 2
    freqs = THETA ** (-np.arange(half, dtype=np.float64) / half)
    freqs = np.concatenate([freqs, freqs])[None, :]
    sign = np.concatenate([-np.ones(half), np.ones(half)])[None, :]
    near = np.arange(ROWS, dtype=np.float64)[:, None] * freqs
    far = (np.arange(prompt_len // ROWS + 1, dtype=np.float64) * ROWS)[:, None] * freqs
    tables = (np.cos(near), np.sin(near) * sign, np.cos(far), np.sin(far) * sign)
    return [t.astype(np.float32) for t in tables]


def pair_lists(chip):
    zz, yy = chip // 2, chip % 2
    at = lambda dz, y: (zz + dz) % 4 * 2 + y
    soon = [at(0, 1 - yy), at(3, yy), at(1, yy), at(2, yy)]
    late = [at(3, 1 - yy), at(1, 1 - yy), at(2, 1 - yy)]
    cut = lambda pairs, limit: [j for j in pairs if j < limit]
    other = (3 - zz) * 2 + yy if chip < 4 else -1
    lists = [cut(soon, chip), cut([chip] + soon, other), cut(late, other), cut(late, chip)]
    return [(len(pairs), sum(j << (3 * k) for k, j in enumerate(pairs))) for pairs in lists]


PAIR_LISTS = [pair_lists(chip) for chip in range(8)]


def pick(index, values):
    result = index * 0 + values[-1]
    for n, value in enumerate(values[:-1]):
        result = result + (index == n).astype(jnp.int32) * (value - values[-1])
    return result


def kernel(
    prompt, gain, w_query, w_key, w_value, q_gain, k_gain, table, ids, near_c, near_s, far_c, far_s, spread,
    out, dec,
    x, wq, wkv, tab, q, kbuf, vbuf, acc, top, es, e0, er, eb, ec, eh, xs, qd, accd, topd, fsend, frecv,
    load_sem, wq_sem, ks, kr, vs, vr, e0r, e1s, e1r, e2s, e2r, e3s, e3r, qs, qr, fs, fr,
):
    ctx = lax.axis_index("ctx")
    tp = lax.axis_index("tp")
    chip = ctx // 2
    core = ctx % 2
    z = ctx // 4
    yh = chip % 2

    def remote(src, dst, send, recv, to_ctx, to_tp):
        return pltpu.make_async_remote_copy(
            src_ref=src, dst_ref=dst, send_sem=send, recv_sem=recv,
            device_id=(to_ctx, to_tp), device_id_type=MESH,
        )

    prompt_loads = []
    for n in range(4):
        rows = pl.ds(n * 128, 128)
        prompt_loads.append(pltpu.make_async_copy(prompt.at[rows], x.at[rows], load_sem.at[n]))
    key_load = pltpu.make_async_copy(w_key, wkv.at[:, pl.ds(0, HD)], load_sem.at[4])
    value_load = pltpu.make_async_copy(w_value, wkv.at[:, pl.ds(HD, HD)], load_sem.at[5])
    table_load = pltpu.make_async_copy(table, tab, load_sem.at[6])
    query_loads = []
    for n in range(2):
        cols = pl.ds((1 - n) * 512, 512)
        query_loads.append(pltpu.make_async_copy(w_query.at[:, cols], wq.at[:, cols], wq_sem.at[n]))
    for load in (*prompt_loads, key_load, value_load):
        load.start()

    barrier = pltpu.get_barrier_semaphore()

    @pl.loop(1, NCTX)
    def _(i):
        pl.semaphore_signal(barrier, inc=1, device_id=((ctx + i) % NCTX, tp), device_id_type=MESH)

    @pl.loop(1, NTP)
    def _(i):
        pl.semaphore_signal(barrier, inc=1, device_id=(ctx, (tp + i) % NTP), device_id_type=MESH)

    def normed(rows_f32):
        mean_square = jnp.mean(rows_f32 * rows_f32, axis=-1, keepdims=True)
        return (rows_f32 * lax.rsqrt(mean_square + EPS) * gain[...]).astype(jnp.bfloat16)

    for n in range(4):
        prompt_loads[n].wait()

        @pl.loop(0, 8, unroll=2)
        def _(i):
            rows = pl.ds(pl.multiple_of(n * 128 + i * 16, 16), 16)
            x[rows, :] = normed(x[rows, :].astype(jnp.float32))

        if n == 2:
            query_loads[0].start()
    query_loads[1].start()
    table_load.start()

    def rotated(raw, head_gain, cosine, sine):
        mean_square = jnp.mean(raw * raw, axis=-1, keepdims=True)
        y = raw * lax.rsqrt(mean_square + EPS) * head_gain
        return (y * cosine + pltpu.roll(y, HD // 2, 1) * sine).astype(jnp.bfloat16)

    base_c, base_s = far_c[pl.ds(ctx, 1), :], far_s[pl.ds(ctx, 1), :]
    cosine = near_c[...] * base_c - near_s[...] * base_s
    sine = near_s[...] * base_c + near_c[...] * base_s

    key_load.wait()
    value_load.wait()
    kv = jnp.dot(x[...], wkv[...], preferred_element_type=jnp.float32)
    kbuf[ctx] = rotated(kv[:, :HD], k_gain[...], cosine, sine)
    vbuf[ctx] = kv[:, HD:].T.astype(jnp.bfloat16)

    pl.semaphore_wait(barrier, NCTX + NTP - 2)

    def block(zz, yy, cc):
        return zz * 4 + yy * 2 + cc

    zp, zm, z2 = (z + 1) % 4, (z + 3) % 4, (z + 2) % 4
    sib = block(z, yh, 1 - core)
    up, down, across = block(zp, yh, core), block(zm, yh, core), block(z, 1 - yh, core)
    late_left, late_right, late_far = (block(n, 1 - yh, core) for n in (zm, zp, z2))
    sent = []

    def block_copy(kind, n, b, to):
        buffer, out_sem, in_sem = (kbuf, ks, kr) if kind == "k" else (vbuf, vs, vr)
        return remote(buffer.at[b], buffer.at[b], out_sem.at[n], in_sem.at[b], to, tp)

    def send(kind, b, to):
        n = sum(1 for item in sent if item[0] == kind)
        block_copy(kind, n, b, to).start()
        sent.append((kind, n, b, to))

    def arrived(kind, b):
        block_copy(kind, 0, b, sib).wait_recv()

    def hop_own():
        send("k", ctx, up)
        send("v", ctx, down)
        send("k", ctx, across)
        send("v", ctx, across)
        send("v", ctx, up)
        send("k", ctx, down)
        send("k", ctx, sib)
        send("v", ctx, sib)

    def hop_ring():
        left, right = block(zm, yh, core), block(zp, yh, core)
        arrived("k", left)
        send("k", left, up)
        arrived("v", right)
        send("v", right, down)
        arrived("v", left)
        arrived("k", right)
        for b in (left, right):
            send("k", b, sib)
            send("v", b, sib)

    def hop_across():
        arrived("k", across)
        arrived("v", across)
        for to in (up, down, sib):
            send("k", across, to)
            send("v", across, to)

    def hop_last(b, *more):
        arrived("k", b)
        arrived("v", b)
        for to in (*more, sib):
            send("k", b, to)
            send("v", b, to)

    def from_sib(zz, yy):
        arrived("k", block(zz, yy, 1 - core))
        arrived("v", block(zz, yy, 1 - core))

    hop_own()

    light = chip < 4
    moved = pick(chip, TAKEN)
    partner = block(3 - z, yh, core)
    kept = jnp.where(light, HEADS, HEADS - moved)

    def project_queries(first):
        raw = jnp.dot(x[...], wq[:, first * HD:(first + 4) * HD], preferred_element_type=jnp.float32)
        for h in range(4):
            q[first + h] = rotated(raw[:, h * HD:(h + 1) * HD], q_gain[...], cosine, sine)

    query_loads[0].wait()
    project_queries(4)

    def query_copy(f):
        return remote(q.at[kept + f], q.at[HEADS + f], qs.at[f], qr.at[f], partner, tp)

    hop_ring()
    query_loads[1].wait()
    project_queries(0)
    hop_across()

    @pl.when(jnp.logical_not(light))
    def _():
        @pl.loop(0, moved)
        def _(f):
            query_copy(f).start()


    def pair_keys(j):
        return kbuf[pl.ds(2 * j, 2)].reshape(PAIR, HD)

    def with_ones(values):
        return jnp.concatenate([values, jnp.ones((16, values.shape[1]), jnp.bfloat16)], axis=0)

    def pair_values(j):
        return with_ones(jnp.concatenate([vbuf[2 * j], vbuf[2 * j + 1]], axis=1))

    def scores(keys, queries):
        return lax.dot_general(keys, queries, (((1,), (1,)), ((), ())), preferred_element_type=jnp.float32)

    def pipeline(units):
        held, mixed = {}, {}
        count = len(units)
        for t in range(count + 2):
            if t < count:
                held[t] = units[t][0]()
            if 0 <= t - 2:
                units[t - 2][2](mixed.pop(t - 2))
            if 0 <= t - 1 < count:
                mixed[t - 1] = units[t - 1][1](held.pop(t - 1))

    def causal(s):
        down = lax.broadcasted_iota(jnp.int32, s.shape, 0)
        return jnp.where(down <= lax.broadcasted_iota(jnp.int32, s.shape, 1), s, LOW)

    def open_unit(source, slot):
        def first():
            return scores(kbuf[ctx], q[source])

        def second(s):
            s = causal(s)
            peak = jnp.max(s, axis=0, keepdims=True) * SCALE
            top[slot, :1, :] = peak
            return jnp.exp2(s * SCALE - peak).astype(jnp.bfloat16)

        def third(w):
            acc[slot] = jnp.dot(with_ones(vbuf[ctx]), w, preferred_element_type=jnp.float32)

        return first, second, third

    def next_unit(keys, values, source, slot, mask=None):
        def first():
            return scores(keys(), q[source])

        def second(s):
            if mask is not None:
                s = mask(s)
            before = top[slot, :1, :]
            peak = jnp.maximum(before, jnp.max(s, axis=0, keepdims=True) * SCALE)
            top[slot, :1, :] = peak
            return jnp.exp2(s * SCALE - peak).astype(jnp.bfloat16), jnp.exp2(before - peak)

        def third(weights):
            w, factor = weights
            acc[slot] = acc[slot] * factor + jnp.dot(values(), w, preferred_element_type=jnp.float32)

        return first, second, third

    def pair_unit(j, source, slot):
        return next_unit(lambda: pair_keys(j), lambda: pair_values(j), source, slot)

    def block_unit(b, source, slot, mask=None):
        return next_unit(lambda: kbuf[b], lambda: with_ones(vbuf[b]), source, slot, mask)

    def open_heads(begin, width, count):
        places = []
        for n in range(width):
            use = n < count
            places.append((jnp.where(use, begin + n, 0), jnp.where(use, begin + n, SPARE)))

        @pl.when(core == 0)
        def _():
            pipeline([open_unit(*place) for place in places])

        @pl.when(core == 1)
        def _():
            pipeline([open_unit(*place) for place in places] + [block_unit(sib, *place) for place in places])

    arrived("k", sib)
    arrived("v", sib)
    hop_last(block(z2, yh, core), across)
    open_heads(chip * 0, 4, kept)

    table_load.wait()
    first_row = (ctx * NTP + tp) * VROWS
    lanes = (lax.broadcasted_iota(jnp.int32, (16, VROWS), 1) + first_row).astype(jnp.float32)
    down = lax.broadcasted_iota(jnp.int32, (16, 16), 0)
    sample = down % 8 * 2 + down // 8
    chosen = sample == lax.broadcasted_iota(jnp.int32, (16, 16), 1)
    picks = []
    for j in range(4):
        wanted = jnp.where(chosen, ids[j:j + 1, :].astype(jnp.float32), 0.0)
        picks.append((jnp.sum(wanted, axis=1, keepdims=True) == lanes).astype(jnp.float32))
    for c in range(2):
        rows = jnp.concatenate([p[c * 8:(c + 1) * 8] for p in picks], axis=0).astype(jnp.bfloat16)
        for n in range(NTP):
            cols = slice(n * PIECE, (n + 1) * PIECE)
            es[c, n] = jnp.dot(rows, tab[:, cols], preferred_element_type=jnp.float32).astype(jnp.bfloat16)

    def core_copy():
        return remote(es.at[1 - core], e0, e1s.at[0], e0r, sib, tp)

    core_copy().start()

    @pl.when(kept > 6)
    def _():
        open_heads(chip * 0 + 4, 4, kept - 4)

    @pl.when(kept <= 6)
    def _():
        open_heads(chip * 0 + 4, 2, kept - 4)

    core_copy().wait_recv()
    for n in range(NTP):
        e0[n] = (e0[n].astype(jnp.float32) + es[core, n].astype(jnp.float32)).astype(jnp.bfloat16)
    er[tp] = e0[tp]

    def token_copy(i, to, frm):
        return remote(e0.at[to], er.at[frm], e1s.at[i], e1r.at[frm], ctx, to)

    @pl.loop(1, NTP)
    def _(i):
        token_copy(i, (tp + i) % NTP, tp).start()

    for zz, yy in ((z, 1 - yh), (zm, yh), (zp, yh), (z2, yh)):
        from_sib(zz, yy)

    @pl.when(light)
    def _():
        @pl.loop(0, moved)
        def _(f):
            acc[HEADS + f] = jnp.zeros((ACC, ROWS), jnp.float32)
            top[HEADS + f] = jnp.full((8, ROWS), LOW, jnp.float32)

    acc[SPARE] = jnp.zeros((ACC, ROWS), jnp.float32)
    top[SPARE] = jnp.zeros((8, ROWS), jnp.float32)

    counts = [pick(chip, [lists[n][0] for lists in PAIR_LISTS]) for n in range(4)]
    codes = [pick(chip, [lists[n][1] for lists in PAIR_LISTS]) for n in range(4)]
    widths = [kept, moved, moved, kept]
    soon_units = counts[0] * kept + counts[1] * moved
    all_units = soon_units + counts[2] * moved + counts[3] * kept
    late_group = soon_units // GROUP

    def choose(turn, values):
        result = values[0]
        for n in range(1, 4):
            result = jnp.where(turn == n, values[n], result)
        return result

    def settle(turn, k, h):
        for n in range(4):
            end = (turn == n) & (k >= counts[n])
            turn = jnp.where(end, n + 1, turn)
            k = jnp.where(end, 0, k)
        return turn, k, h

    def sample_copy(i, to, frm):
        return remote(eb.at[to], ec.at[frm], e2s.at[i], e2r.at[frm], to * 2 + core, tp)

    def sum_tokens():
        @pl.loop(1, NTP)
        def _(i):
            frm = (tp + i) % NTP
            token_copy(i, frm, frm).wait_recv()

        piece = er[0].astype(jnp.float32)
        for n in range(1, NTP):
            piece = piece + er[n].astype(jnp.float32)
        piece = jnp.dot(spread[...], piece.astype(jnp.bfloat16), preferred_element_type=jnp.float32)
        eb[...] = piece.astype(jnp.bfloat16).reshape(8, 16, PIECE)
        ec[chip] = eb[chip]

        @pl.loop(1, 8)
        def _(i):
            sample_copy(i, (chip + i) % 8, chip).start()

    def piece_copy(i, to, frm):
        return remote(eh.at[frm], eh.at[frm], e3s.at[i], e3r.at[frm], ctx, to)

    def sum_samples():
        @pl.loop(1, 8)
        def _(i):
            frm = (chip + i) % 8
            sample_copy(i, frm, frm).wait_recv()

        piece = ec[0].astype(jnp.float32)
        for n in range(1, 8):
            piece = piece + ec[n].astype(jnp.float32)
        eh[tp] = piece.astype(jnp.bfloat16)

        @pl.loop(1, NTP)
        def _(i):
            piece_copy(i, (tp + i) % NTP, tp).start()

    def between(g):
        @pl.when(light & (g == jnp.minimum(chip, 1)))
        def _():
            @pl.loop(0, moved)
            def _(f):
                query_copy(f).wait_recv()

        @pl.when(g == 1)
        def _():
            hop_last(late_left)
            hop_last(late_right)
            hop_last(late_far)

        @pl.when(g == 2)
        def _():
            sum_tokens()

        @pl.when(g == late_group)
        def _():
            for zz in (zm, zp, z2):
                from_sib(zz, 1 - yh)

        @pl.when(g == late_group + 1)
        def _():
            sum_samples()

    def step(g, state):
        between(g)
        units = []
        for n in range(GROUP):
            turn, k, h = state
            use = turn < 4
            j = lax.shift_right_logical(choose(turn, codes), 3 * k) % 8
            slot = h + jnp.where((turn == 1) | (turn == 2), HEADS, 0 * h)
            units.append(pair_unit(jnp.where(use, j, chip), jnp.where(use, slot, 0), jnp.where(use, slot, SPARE)))
            h = h + 1
            wrap = h >= choose(turn, widths)
            state = settle(turn, k + wrap.astype(jnp.int32), jnp.where(wrap, 0, h))
        pipeline(units)
        return state

    lax.fori_loop(0, (all_units + GROUP - 1) // GROUP, step, settle(chip * 0, chip * 0, chip * 0))

    def finished(slot):
        mix = acc[slot]
        return (mix[:HD] * (1.0 / mix[HD:HD + 1])).T.astype(jnp.bfloat16)

    def result_copy(f):
        return remote(fsend.at[f], frecv.at[f], fs.at[f], fr.at[f], partner, tp)

    @pl.when(light)
    def _():
        def close_heads(width):
            places = []
            for f in range(width):
                use = f < moved
                slot = HEADS + f + 0 * chip
                places.append((jnp.where(use, slot, 0), jnp.where(use, slot, SPARE)))

            @pl.when(core == 0)
            def _():
                pipeline([block_unit(partner, *place, causal) for place in places])

            @pl.when(core == 1)
            def _():
                pipeline(
                    [block_unit(partner, *place, causal) for place in places]
                    + [block_unit(partner - 1, *place) for place in places]
                )

        @pl.when(moved == 1)
        def _():
            close_heads(1)

        @pl.when(moved > 1)
        def _():
            close_heads(3)

        @pl.loop(0, moved)
        def _(f):
            fsend[f] = finished(HEADS + f)
            result_copy(f).start()

    @pl.loop(1, NTP)
    def _(i):
        frm = (tp + i) % NTP
        piece_copy(i, frm, frm).wait_recv()

    hidden = jnp.concatenate([eh[n] for n in range(NTP)], axis=1).astype(jnp.float32)
    xs[...] = normed(hidden)
    step_c, step_s = far_c[NCTX:NCTX + 1, :], far_s[NCTX:NCTX + 1, :]
    dec_c = near_c[:16, :] * step_c - near_s[:16, :] * step_s
    dec_s = near_s[:16, :] * step_c + near_c[:16, :] * step_s
    step_kv = jnp.dot(xs[...], wkv[...], preferred_element_type=jnp.float32)
    step_k = rotated(step_kv[:, :HD], k_gain[...], dec_c, dec_s)
    step_v = step_kv[:, HD:].astype(jnp.bfloat16)
    for g in range(2):
        raw = jnp.dot(xs[...], wq[:, g * 512:(g + 1) * 512], preferred_element_type=jnp.float32)
        for h in range(4):
            rows = slice((g * 4 + h) * 16, (g * 4 + h + 1) * 16)
            qd[rows, :] = rotated(raw[:, h * HD:(h + 1) * HD], q_gain[...], dec_c, dec_s)

    own = scores(step_k, qd[...])
    step = lax.broadcasted_iota(jnp.int32, (16, HD), 1) % 16
    own = jnp.where(lax.broadcasted_iota(jnp.int32, (16, HD), 0) <= step, own, LOW)
    peak = jnp.max(own, axis=0, keepdims=True) * SCALE
    weights = jnp.exp2(own * SCALE - peak).astype(jnp.bfloat16)
    topd[:1, :] = peak
    step_values = jnp.concatenate([step_v, jnp.ones((16, 16), jnp.bfloat16)], axis=1)
    accd[...] = lax.dot_general(
        step_values, weights, (((0,), (0,)), ((), ())), preferred_element_type=jnp.float32
    )

    def step_unit(j):
        def first():
            return scores(kbuf[4 * j:4 * j + 4].reshape(2 * PAIR, HD), qd[...])

        def second(s):
            before = topd[:1, :]
            peak = jnp.maximum(before, jnp.max(s, axis=0, keepdims=True) * SCALE)
            topd[:1, :] = peak
            return jnp.exp2(s * SCALE - peak).astype(jnp.bfloat16), jnp.exp2(before - peak)

        def third(weights):
            w, factor = weights
            values = with_ones(jnp.concatenate([vbuf[4 * j + n] for n in range(4)], axis=1))
            accd[...] = accd[...] * factor + jnp.dot(values, w, preferred_element_type=jnp.float32)

        return first, second, third

    pipeline([step_unit(j) for j in range(4)])
    mix = accd[...]
    steps = (mix[:HD] * (1.0 / mix[HD:HD + 1])).T.astype(jnp.bfloat16)
    for h in range(HEADS):
        dec[:, h * HD:(h + 1) * HD] = steps[h * 16:(h + 1) * 16, :]

    @pl.loop(0, kept)
    def _(h):
        out[:, pl.ds(pl.multiple_of(h * HD, HD), HD)] = finished(h)

    @pl.when(jnp.logical_not(light))
    def _():
        @pl.loop(0, moved)
        def _(f):
            result_copy(f).wait_recv()
            out[:, pl.ds(pl.multiple_of((kept + f) * HD, HD), HD)] = frecv[f]
            query_copy(f).wait_send()

    @pl.when(light)
    def _():
        @pl.loop(0, moved)
        def _(f):
            result_copy(f).wait_send()

    for item in sent:
        block_copy(*item).wait_send()

    core_copy().wait_send()

    @pl.loop(1, NTP)
    def _(i):
        to = (tp + i) % NTP
        token_copy(i, to, tp).wait_send()
        piece_copy(i, to, tp).wait_send()

    @pl.loop(1, 8)
    def _(i):
        sample_copy(i, (chip + i) % 8, chip).wait_send()


def body(prompt, norm_gain, w_query, w_key, w_value, query_gain, key_gain, table, sampled):
    near_c, near_s, far_c, far_s = rope_tables(NCTX * ROWS)
    spread = np.zeros((8 * 16, 32), np.float32)
    for s in range(8):
        for j in range(4):
            spread[s * 16 + j, j * 8 + s] = 1.0
    hbm = pl.BlockSpec(memory_space=pl.ANY)
    vmem = pl.BlockSpec(memory_space=pltpu.VMEM)
    bf, f32 = jnp.bfloat16, jnp.float32
    dma = pltpu.SemaphoreType.DMA
    out, dec = pl.pallas_call(
        kernel,
        out_shape=(
            jax.ShapeDtypeStruct((ROWS, HEADS * HD), bf),
            jax.ShapeDtypeStruct((16, HEADS * HD), bf),
        ),
        in_specs=[hbm, vmem, hbm, hbm, hbm, vmem, vmem, hbm] + [vmem] * 6,
        out_specs=(vmem, vmem),
        scratch_shapes=[
            pltpu.VMEM((ROWS, D), bf),
            pltpu.VMEM((D, HEADS * HD), bf),
            pltpu.VMEM((D, 2 * HD), bf),
            pltpu.VMEM((VROWS, D), bf),
            pltpu.VMEM((12, ROWS, HD), bf),
            pltpu.VMEM((NCTX, ROWS, HD), bf),
            pltpu.VMEM((NCTX, HD, ROWS), bf),
            pltpu.VMEM((SPARE + 1, ACC, ROWS), f32),
            pltpu.VMEM((SPARE + 1, 8, ROWS), f32),
            pltpu.VMEM((2, NTP, 32, PIECE), bf),
            pltpu.VMEM((NTP, 32, PIECE), bf),
            pltpu.VMEM((NTP, 32, PIECE), bf),
            pltpu.VMEM((8, 16, PIECE), bf),
            pltpu.VMEM((8, 16, PIECE), bf),
            pltpu.VMEM((NTP, 16, PIECE), bf),
            pltpu.VMEM((16, D), bf),
            pltpu.VMEM((HD, HD), bf),
            pltpu.VMEM((ACC, HD), f32),
            pltpu.VMEM((8, HD), f32),
            pltpu.VMEM((4, ROWS, HD), bf),
            pltpu.VMEM((4, ROWS, HD), bf),
            dma((7,)), dma((2,)),
            dma((16,)), dma((NCTX,)), dma((16,)), dma((NCTX,)),
            dma, dma((NTP,)), dma((NTP,)), dma((8,)), dma((8,)), dma((NTP,)), dma((NTP,)),
            dma((4,)), dma((4,)), dma((4,)), dma((4,)),
        ],
        compiler_params=pltpu.CompilerParams(
            collective_id=0, has_side_effects=True, vmem_limit_bytes=62 * 2**20
        ),
    )(
        prompt, norm_gain[None, :], w_query, w_key, w_value, query_gain[None, :], key_gain[None, :], table,
        sampled.T, near_c, near_s, far_c, far_s, spread.astype(jnp.bfloat16),
    )
    return out, dec[None, :4]


def solution(mesh):
    in_specs = (
        P("ctx", None),
        P(),
        P(None, "tp"),
        P(None, "tp"),
        P(None, "tp"),
        P(),
        P(),
        P(("ctx", "tp"), None),
        P(),
    )
    out_specs = (P("ctx", "tp"), P("ctx", None, "tp"))
    return jax.shard_map(body, mesh=mesh, in_specs=in_specs, out_specs=out_specs, check_vma=False)
```
